256 devices in a mesh: replica: 8 (over z_lo, y), slab: 8 (over z_hi, core), heads: 4 (over x).
Axes of the slice: x: 4, y: 4, z: 8 (z_hi: 4, z_lo: 2; z = z_hi * 2 + z_lo), core: 2. Of those that a mesh axis runs over, the one named last changes fastest.
Arguments:
- q_video: bfloat16 [32768, 3072], P(('replica', 'slab', 'heads')), parts along dimension 0, may hold values from -6 to 6
- k_video: bfloat16 [32768, 3072], P(('replica', 'slab', 'heads')), parts along dimension 0, may hold values from -6 to 6
- v_video: bfloat16 [32768, 3072], P(('replica', 'slab', 'heads')), parts along dimension 0, may hold values from -6 to 6
- cot_video: bfloat16 [32768, 3072], P(('replica', 'slab', 'heads')), parts along dimension 0, may hold values from -6 to 6
- q_text: bfloat16 [2048, 3072], P(('replica', 'slab', 'heads')), parts along dimension 0, may hold values from -6 to 6
- k_text: bfloat16 [2048, 3072], P(('replica', 'slab', 'heads')), parts along dimension 0, may hold values from -6 to 6
- v_text: bfloat16 [2048, 3072], P(('replica', 'slab', 'heads')), parts along dimension 0, may hold values from -6 to 6
- cot_text: bfloat16 [2048, 3072], P(('replica', 'slab', 'heads')), parts along dimension 0, may hold values from -6 to 6
- gain_qv: float32 [1024], P('replica'), parts along dimension 0, may hold values from 0.5 to 5
- gain_kv: float32 [1024], P('replica'), parts along dimension 0, may hold values from 0.5 to 5
- gain_qt: float32 [1024], P('replica'), parts along dimension 0, may hold values from 0.5 to 5
- gain_kt: float32 [1024], P('replica'), parts along dimension 0, may hold values from 0.5 to 5
- windows: int32 [24, 3], replicated, may hold values from 1 to 3, as said below
- text_mask: int32 [2048], P('replica'), parts along dimension 0, may hold values from 0 to 1, as said below
Outputs:
- out_video: bfloat16 [32768, 3072], P(('replica', 'slab', 'heads')), parts along dimension 0
- out_text: bfloat16 [2048, 3072], P(('replica', 'slab', 'heads')), parts along dimension 0
- dq_video: bfloat16 [32768, 3072], P(('replica', 'slab', 'heads')), parts along dimension 0
- dk_video: bfloat16 [32768, 3072], P(('replica', 'slab', 'heads')), parts along dimension 0
- dv_video: bfloat16 [32768, 3072], P(('replica', 'slab', 'heads')), parts along dimension 0
- dq_text: bfloat16 [2048, 3072], P(('replica', 'slab', 'heads')), parts along dimension 0
- dk_text: bfloat16 [2048, 3072], P(('replica', 'slab', 'heads')), parts along dimension 0
- dv_text: bfloat16 [2048, 3072], P(('replica', 'slab', 'heads')), parts along dimension 0
- grad_gain_qv: float32 [1024], P('replica'), parts along dimension 0
- grad_gain_kv: float32 [1024], P('replica'), parts along dimension 0
- grad_gain_qt: float32 [1024], P('replica'), parts along dimension 0
- grad_gain_kt: float32 [1024], P('replica'), parts along dimension 0
The draws below stay inside these ranges and needn't reach their ends.
There are 8 independent parts, one for each index of `replica`. The reference program is written for one: setup_inputs(seed, part) draws one part's arguments, and reference() takes and returns one part's arrays. A program takes and returns all parts, laid end to end along the dimension named above; an argument that names none is the same for every part. Nothing has to cross between parts.
Inputs may be any that keep to these rules, and one draw needn't show every extreme that they name: `windows`: every entry is 1 or 3; half of the heads have 3 along time. `text_mask`: A leading run of at least 64 ones, then zeros; the last entry is 0.
All inputs are finite; a program needn't handle non-finite values.
Results may differ from the reference program's by a relative error of at most 0.04.
The reference program's roundings to bfloat16 on the way count: a program that leaves them out, or rounds other values in their place, can miss the bound.
Values may be sent and summed in bfloat16 or wider, within the bound.
A program may use at most 192 MiB of HBM per device.

```python
import jax
import jax.numpy as jnp
from jax import lax

HEADS = 24
HD = 128
D = 3072
TEXT = 256
GRID_H = 16
GRID_W = 32
TOKENS = 4096
N_SLAB = 8


def draw_q_video(key, part):
    key = jax.random.fold_in(key, 1)
    values = jax.random.normal(key, (TOKENS, D), jnp.float32)
    return jnp.clip(values, -6.0, 6.0).astype(jnp.bfloat16)


def draw_k_video(key, part):
    key = jax.random.fold_in(key, 2)
    values = jax.random.normal(key, (TOKENS, D), jnp.float32)
    return jnp.clip(values, -6.0, 6.0).astype(jnp.bfloat16)


def draw_q_text(key, part):
    key = jax.random.fold_in(key, 3)
    values = jax.random.normal(key, (TEXT, D), jnp.float32)
    return jnp.clip(values, -6.0, 6.0).astype(jnp.bfloat16)


def draw_k_text(key, part):
    key = jax.random.fold_in(key, 4)
    values = jax.random.normal(key, (TEXT, D), jnp.float32)
    return jnp.clip(values, -6.0, 6.0).astype(jnp.bfloat16)


def gain_values(key, salt):
    return jnp.exp(jax.random.uniform(jax.random.fold_in(key, salt), (HD,), jnp.float32, jnp.log(0.5), jnp.log(2.0)))


def draw_gain_qv(key, part):
    key = jax.random.fold_in(key, 11)
    spread = gain_values(key, 1)
    return spread


def draw_gain_kv(key, part):
    key = jax.random.fold_in(key, 12)
    spread = gain_values(key, 1)
    return spread


def draw_gain_qt(key, part):
    key = jax.random.fold_in(key, 13)
    spread = gain_values(key, 1)
    return spread


def draw_gain_kt(key, part):
    key = jax.random.fold_in(key, 14)
    spread = gain_values(key, 1)
    return spread


def draw_windows(key, part):
    key = jax.random.fold_in(key, 31)
    shuffle = jax.random.permutation(jax.random.fold_in(key, 1), HEADS)
    reach_time = 1 + 2 * (shuffle < HEADS // 2).astype(jnp.int32)
    reach_space = 1 + 2 * jax.random.randint(jax.random.fold_in(key, 2), (HEADS, 2), 0, 2)
    return jnp.concatenate([reach_time[:, None], reach_space], axis=1).astype(jnp.int32)


def draw_text_mask(key, part):
    key = jax.random.fold_in(key, 41)
    length = jax.random.randint(key, (), TEXT // 4, TEXT)
    return (jnp.arange(TEXT) < length).astype(jnp.int32)


def block_scale(key, dims, shards, smallest, top_value):
    def one(axis_at, shards_of):
        steps = jax.random.uniform(jax.random.fold_in(jax.random.fold_in(key, 6), axis_at), (shards_of,), jnp.float32, smallest / len(shards), top_value / len(shards))
        return jnp.repeat(jnp.exp(steps), dims[axis_at] // shards_of).reshape((-1,) + (1,) * (len(dims) - axis_at - 1))

    loudness = one(*shards[0])
    for cut in shards[1:]:
        loudness = loudness * one(*cut)
    return loudness


def normal_values(own_key, shape, width, limit, shards=(), kind=jnp.bfloat16):
    loudness = block_scale(own_key, shape, shards, -0.22, 0.18) if shards else 1.0
    entries = jax.random.normal(own_key, shape, jnp.float32) * width * loudness
    return jnp.minimum(jnp.maximum(entries, -limit), limit).astype(kind)


def setup_inputs(seed: int = 0, part: int = 0) -> dict:
    keys = jax.random.split(jax.random.key(seed), 15)
    part_splits = jax.random.split(jax.random.fold_in(keys[14], part), 15)
    return {
        "q_video": draw_q_video(jax.random.fold_in(jax.random.fold_in(keys[14], part), 71), part),
        "k_video": draw_k_video(jax.random.fold_in(jax.random.fold_in(keys[14], part), 71), part),
        "v_video": normal_values(part_splits[2], (TOKENS, D), 1.0, 6.0, ((0, 32),)),
        "cot_video": normal_values(part_splits[3], (TOKENS, D), 1.0, 6.0, ((0, 32),)),
        "q_text": draw_q_text(jax.random.fold_in(jax.random.fold_in(keys[14], part), 71), part),
        "k_text": draw_k_text(jax.random.fold_in(jax.random.fold_in(keys[14], part), 71), part),
        "v_text": normal_values(part_splits[6], (TEXT, D), 1.0, 6.0, ((0, 32),)),
        "cot_text": normal_values(part_splits[7], (TEXT, D), 1.0, 6.0, ((0, 32),)),
        "gain_qv": draw_gain_qv(jax.random.fold_in(jax.random.fold_in(keys[14], part), 71), part),
        "gain_kv": draw_gain_kv(jax.random.fold_in(jax.random.fold_in(keys[14], part), 71), part),
        "gain_qt": draw_gain_qt(jax.random.fold_in(jax.random.fold_in(keys[14], part), 71), part),
        "gain_kt": draw_gain_kt(jax.random.fold_in(jax.random.fold_in(keys[14], part), 71), part),
        "windows": draw_windows(jax.random.fold_in(keys[14], 71), part),
        "text_mask": draw_text_mask(jax.random.fold_in(jax.random.fold_in(keys[14], part), 71), part),
    }


EPSILON = 1e-06
ROPE_BASE = 256.0
NEGATIVE = -1e+30

def section_list(head_dim):
    first_len = head_dim // 8
    other_len = 7 * head_dim // 16
    return ((0, first_len), (first_len, other_len), (first_len + other_len, other_len))

def rope_tables(token_index, head_dim):
    frame_at = token_index // (GRID_H * GRID_W)
    height = token_index // GRID_W % GRID_H
    across = token_index % GRID_W
    places = (frame_at, height, across)
    angles = []
    for number, (start_offset, length) in enumerate(section_list(head_dim)):
        half_len = length // 2
        offsets = (jnp.arange(length, dtype=jnp.int32) % half_len).astype(jnp.float32)
        frequency = jnp.power(jnp.float32(ROPE_BASE), -2.0 * offsets / length)
        angles.append(places[number].astype(jnp.float32)[:, None] * frequency[None, :])
    angles = jnp.concatenate(angles, axis=1)
    return (jnp.cos(angles), jnp.sin(angles))

def swap_halves(values, head_dim):
    pieces = []
    for start_offset, length in section_list(head_dim):
        half_len = length // 2
        pieces.append(-values[..., start_offset + half_len:start_offset + length])
        pieces.append(values[..., start_offset:start_offset + half_len])
    return jnp.concatenate(pieces, axis=-1)

def rotate(values, cosine_tab, sine_tab, head_dim):
    return values * cosine_tab[:, None, :] + swap_halves(values, head_dim) * sine_tab[:, None, :]

def unit_rows(source, head_count):
    values = source.astype(jnp.float32).reshape(source.shape[0], head_count, HD)
    inverse = lax.rsqrt(lax.optimization_barrier(jnp.mean(values * values, axis=-1, keepdims=True)) + EPSILON)
    return (values * inverse, inverse)

def norm_back(grad_out, normed, inverse, gain):
    scaled = grad_out * gain
    grad_in = inverse * (scaled - normed * lax.optimization_barrier(jnp.mean(scaled * normed, axis=-1, keepdims=True)))
    return (grad_in, lax.optimization_barrier(jnp.sum(grad_out * normed, axis=(0, 1))))

def matmul(first_op, second_op):
    return jnp.dot(first_op, second_op, preferred_element_type=jnp.float32)

def contract_last(first_op, second_op):
    return lax.dot_general(first_op, second_op, (((1,), (1,)), ((), ())), preferred_element_type=jnp.float32)

def contract_leading_axes(first_op, second_op):
    return lax.dot_general(first_op, second_op, (((0,), (0,)), ((), ())), preferred_element_type=jnp.float32)

def tile_places(band_token_count):
    per_frame = GRID_H * GRID_W
    query_pos = jnp.arange(band_token_count, dtype=jnp.int32)
    key_pos = jnp.arange(3 * band_token_count, dtype=jnp.int32)
    key_local = key_pos % band_token_count
    key_shift = key_pos // band_token_count - 1
    q_row = query_pos % per_frame // GRID_W // 8
    q_col = query_pos % GRID_W // 8
    k_row = key_local % per_frame // GRID_W // 8
    k_col = key_local % GRID_W // 8
    return (q_row, q_col, k_row, k_col, key_shift)

def window_mask(places, extent, slab_at, slab_total):
    q_row, q_col, k_row, k_col, key_shift = places
    exists = (slab_at + key_shift >= 0) & (slab_at + key_shift < slab_total)
    in_time = (jnp.abs(key_shift) <= extent[0] // 2) & exists
    rows_ok = jnp.abs(q_row[:, None] - k_row[None, :]) <= extent[1] // 2
    cols_ok = jnp.abs(q_col[:, None] - k_col[None, :]) <= extent[2] // 2
    return in_time[None, :] & rows_ok & cols_ok

def block_attend(queries, key_rows, value_rows, grad_rows, text_keys, text_values, allowed, usable, factor):
    scores_video = jnp.where(allowed, contract_last(queries, key_rows) * factor, NEGATIVE)
    scores_text = jnp.where(usable[None, :], contract_last(queries, text_keys) * factor, NEGATIVE)
    row_top = jnp.maximum(lax.optimization_barrier(jnp.max(scores_video, axis=1)), lax.optimization_barrier(jnp.max(scores_text, axis=1)))[:, None]
    exp_video = jnp.exp(scores_video - row_top)
    exp_text = jnp.exp(scores_text - row_top)
    row_sum = (lax.optimization_barrier(jnp.sum(exp_video, axis=1)) + lax.optimization_barrier(jnp.sum(exp_text, axis=1)))[:, None]
    video_weight = exp_video.astype(jnp.bfloat16)
    weight_text = exp_text.astype(jnp.bfloat16)
    outputs = ((matmul(video_weight, value_rows) + matmul(weight_text, text_values)) / row_sum).astype(jnp.bfloat16)
    row_dot = lax.optimization_barrier(jnp.sum(grad_rows.astype(jnp.float32) * outputs.astype(jnp.float32), axis=1, keepdims=True))
    slope_video = (exp_video / row_sum * (contract_last(grad_rows, value_rows) - row_dot)).astype(jnp.bfloat16)
    slope_text = (exp_text / row_sum * (contract_last(grad_rows, text_values) - row_dot)).astype(jnp.bfloat16)
    query_gradient = factor * (matmul(slope_video, key_rows) + matmul(slope_text, text_keys))
    grad_k = factor * contract_leading_axes(slope_video, queries)
    value_gradient = contract_leading_axes(video_weight, grad_rows)
    text_key_gradient = factor * contract_leading_axes(slope_text, queries)
    text_value_gradient = contract_leading_axes(weight_text, grad_rows)
    return (outputs, query_gradient, grad_k, value_gradient, text_key_gradient, text_value_gradient)

def reference(q_video, k_video, v_video, cot_video, q_text, k_text, v_text, cot_text, gain_qv, gain_kv, gain_qt, gain_kt, windows, text_mask):
    factor = HD ** (-0.5)
    combined_tokens = q_video.shape[0]
    band_token_count = combined_tokens // N_SLAB
    token_index = jnp.arange(combined_tokens, dtype=jnp.int32)
    cosine_tab, sine_tab = rope_tables(token_index, HD)
    q_unit, q_inverse = unit_rows(q_video, HEADS)
    k_unit, k_inverse = unit_rows(k_video, HEADS)
    q_norm = rotate(q_unit * gain_qv, cosine_tab, sine_tab, HD).astype(jnp.bfloat16)
    k_norm = rotate(k_unit * gain_kv, cosine_tab, sine_tab, HD).astype(jnp.bfloat16)
    qt_unit, qt_inverse = unit_rows(q_text, HEADS)
    kt_unit, kt_inverse = unit_rows(k_text, HEADS)
    qt_norm = (qt_unit * gain_qt).astype(jnp.bfloat16)
    kt_norm = (kt_unit * gain_kt).astype(jnp.bfloat16)
    usable = text_mask == 1
    places = tile_places(band_token_count)

    def heads_first(source):
        return source.reshape(source.shape[0], HEADS, HD).transpose(1, 0, 2)

    def per_head(packed):
        q_one, k_one, v_one, g_one, qt_one, kt_one, vt_one, text_gain_single, extent = packed
        zero_pad = jnp.zeros((band_token_count, HD), jnp.bfloat16)
        k_padded = jnp.concatenate([zero_pad, k_one, zero_pad], axis=0)
        v_padded = jnp.concatenate([zero_pad, v_one, zero_pad], axis=0)

        def band_advance(block_at, carried_state):
            output_rows, query_gradient, padded_key_gradient, padded_value_gradient, text_key_gradient, text_value_gradient = carried_state
            start_offset = (block_at * band_token_count).astype(jnp.int32)
            allowed = window_mask(places, extent, block_at, N_SLAB)
            final_result = block_attend(lax.dynamic_slice_in_dim(q_one, start_offset, band_token_count, 0), lax.dynamic_slice_in_dim(k_padded, start_offset, 3 * band_token_count, 0), lax.dynamic_slice_in_dim(v_padded, start_offset, 3 * band_token_count, 0), lax.dynamic_slice_in_dim(g_one, start_offset, band_token_count, 0), kt_one, vt_one, allowed, usable, factor)
            output_rows = lax.dynamic_update_slice_in_dim(output_rows, final_result[0], start_offset, 0)
            query_gradient = lax.dynamic_update_slice_in_dim(query_gradient, final_result[1], start_offset, 0)
            padded_key_gradient = lax.dynamic_update_slice_in_dim(padded_key_gradient, lax.dynamic_slice_in_dim(padded_key_gradient, start_offset, 3 * band_token_count, 0) + final_result[2], start_offset, 0)
            padded_value_gradient = lax.dynamic_update_slice_in_dim(padded_value_gradient, lax.dynamic_slice_in_dim(padded_value_gradient, start_offset, 3 * band_token_count, 0) + final_result[3], start_offset, 0)
            return (output_rows, query_gradient, padded_key_gradient, padded_value_gradient, text_key_gradient + final_result[4], text_value_gradient + final_result[5])
        initial_state = (jnp.zeros((combined_tokens, HD), jnp.bfloat16), jnp.zeros((combined_tokens, HD), jnp.float32), jnp.zeros((combined_tokens + 2 * band_token_count, HD), jnp.float32), jnp.zeros((combined_tokens + 2 * band_token_count, HD), jnp.float32), jnp.zeros((TEXT, HD), jnp.float32), jnp.zeros((TEXT, HD), jnp.float32))
        output_rows, query_gradient, padded_key_gradient, padded_value_gradient, text_key_gradient, text_value_gradient = lax.fori_loop(0, N_SLAB, band_advance, initial_state)
        scores_video = contract_last(qt_one, k_one) * factor
        scores_text = jnp.where(usable[None, :], contract_last(qt_one, kt_one) * factor, NEGATIVE)
        row_top = jnp.maximum(lax.optimization_barrier(jnp.max(scores_video, axis=1)), lax.optimization_barrier(jnp.max(scores_text, axis=1)))[:, None]
        exp_video = jnp.exp(scores_video - row_top)
        exp_text = jnp.exp(scores_text - row_top)
        row_sum = (lax.optimization_barrier(jnp.sum(exp_video, axis=1)) + lax.optimization_barrier(jnp.sum(exp_text, axis=1)))[:, None]
        video_weight = exp_video.astype(jnp.bfloat16)
        weight_text = exp_text.astype(jnp.bfloat16)
        out_text_one = ((matmul(video_weight, v_one) + matmul(weight_text, vt_one)) / row_sum).astype(jnp.bfloat16)
        row_dot = lax.optimization_barrier(jnp.sum(text_gain_single.astype(jnp.float32) * out_text_one.astype(jnp.float32), axis=1, keepdims=True))
        slope_video = (exp_video / row_sum * (contract_last(text_gain_single, v_one) - row_dot)).astype(jnp.bfloat16)
        slope_text = (exp_text / row_sum * (contract_last(text_gain_single, vt_one) - row_dot)).astype(jnp.bfloat16)
        grad_qt = factor * (matmul(slope_video, k_one) + matmul(slope_text, kt_one))
        grad_k = padded_key_gradient[band_token_count:band_token_count + combined_tokens] + factor * contract_leading_axes(slope_video, qt_one)
        value_gradient = padded_value_gradient[band_token_count:band_token_count + combined_tokens] + contract_leading_axes(video_weight, text_gain_single)
        text_key_gradient = text_key_gradient + factor * contract_leading_axes(slope_text, qt_one)
        text_value_gradient = text_value_gradient + contract_leading_axes(weight_text, text_gain_single)
        return (output_rows, query_gradient, grad_k, value_gradient, out_text_one, grad_qt, text_key_gradient, text_value_gradient)
    outputs = lax.map(per_head, (heads_first(q_norm), heads_first(k_norm), heads_first(v_video), heads_first(cot_video), heads_first(qt_norm), heads_first(kt_norm), heads_first(v_text), heads_first(cot_text), windows))
    out_heads, query_gradient, grad_k, value_gradient, out_text_h, grad_qt, text_key_gradient, text_value_gradient = outputs

    def tokens_first(source):
        return source.transpose(1, 0, 2)

    def rounded(source):
        return lax.optimization_barrier(tokens_first(source).astype(jnp.bfloat16)).astype(jnp.float32)
    out_video = tokens_first(out_heads).reshape(combined_tokens, D)
    out_text = tokens_first(out_text_h).reshape(TEXT, D)
    dq_in, grad_gain_qv = norm_back(rotate(rounded(query_gradient), cosine_tab, -sine_tab, HD), q_unit, q_inverse, gain_qv)
    dk_in, grad_gain_kv = norm_back(rotate(rounded(grad_k), cosine_tab, -sine_tab, HD), k_unit, k_inverse, gain_kv)
    dqt_in, grad_gain_qt = norm_back(rounded(grad_qt), qt_unit, qt_inverse, gain_qt)
    dkt_in, grad_gain_kt = norm_back(rounded(text_key_gradient), kt_unit, kt_inverse, gain_kt)
    dq_video = dq_in.reshape(combined_tokens, D).astype(jnp.bfloat16)
    dk_video = dk_in.reshape(combined_tokens, D).astype(jnp.bfloat16)
    dv_video = tokens_first(value_gradient).reshape(combined_tokens, D).astype(jnp.bfloat16)
    dq_text = dqt_in.reshape(TEXT, D).astype(jnp.bfloat16)
    dk_text = dkt_in.reshape(TEXT, D).astype(jnp.bfloat16)
    dv_text = tokens_first(text_value_gradient).reshape(TEXT, D).astype(jnp.bfloat16)
    return (out_video, out_text, dq_video, dk_video, dv_video, dq_text, dk_text, dv_text, grad_gain_qv, grad_gain_kv, grad_gain_qt, grad_gain_kt)
```

```python
import functools

import jax
import jax.numpy as jnp
from jax import lax
from jax.experimental import pallas as pl
from jax.experimental.pallas import tpu as pltpu
from jax.sharding import PartitionSpec as P

HEADS = 24
HD = 128
D = 3072
TEXT = 256
GRID_H = 16
GRID_W = 32

EPSILON = 1e-06
ROPE_BASE = 256.0
NEGATIVE = -1e30
FACTOR = HD ** (-0.5)
LOG2E = 1.4426950408889634
SHARP = FACTOR * LOG2E
MESH = pl.DeviceIdType.MESH
F32 = jnp.float32
BF16 = jnp.bfloat16


def section_list(head_dim):
    first_len = head_dim // 8
    other_len = 7 * head_dim // 16
    return ((0, first_len), (first_len, other_len), (first_len + other_len, other_len))


def rope_tables(token_index, head_dim):
    frame_at = token_index // (GRID_H * GRID_W)
    height = token_index // GRID_W % GRID_H
    across = token_index % GRID_W
    places = (frame_at, height, across)
    angles = []
    signs = []
    for number, (start_offset, length) in enumerate(section_list(head_dim)):
        half_len = length // 2
        offsets = (jnp.arange(length, dtype=jnp.int32) % half_len).astype(jnp.float32)
        frequency = jnp.power(jnp.float32(ROPE_BASE), -2.0 * offsets / length)
        angles.append(places[number].astype(jnp.float32)[:, None] * frequency[None, :])
        signs.append(jnp.where(jnp.arange(length) < half_len, -1.0, 1.0))
    angles = jnp.concatenate(angles, axis=1)
    signs = jnp.concatenate(signs)[None, :]
    return jnp.cos(angles), jnp.sin(angles) * signs


def head_order(windows, groups):
    local = HEADS // groups
    wide = windows[:, 0] == 3
    ids = jnp.arange(HEADS, dtype=jnp.int32)
    before = ids[None, :] < ids[:, None]
    rank_wide = jnp.sum(before & wide[None, :], axis=1, dtype=jnp.int32)
    rank_flat = jnp.sum(before & ~wide[None, :], axis=1, dtype=jnp.int32)
    slot = jnp.where(wide, rank_wide // groups, local // 2 + rank_flat // groups)
    group = jnp.where(wide, rank_wide % groups, rank_flat % groups)
    place = group * local + slot
    chosen = place[None, :] == ids[:, None]
    order = jnp.sum(jnp.where(chosen, ids[None, :], 0), axis=1, dtype=jnp.int32)
    reach = windows[:, 1:] // 2
    reach = jnp.sum(jnp.where(chosen[:, :, None], reach[None, :, :], 0), axis=1, dtype=jnp.int32)
    return order, place, reach.reshape(2 * HEADS)


def nt(a, b):
    return lax.dot_general(a, b, (((1,), (1,)), ((), ())), preferred_element_type=F32)


def nn(a, b):
    return lax.dot_general(a, b, (((1,), (0,)), ((), ())), preferred_element_type=F32)


def fold(values, op):
    return op(values.reshape(values.shape[0] // 8, 8, values.shape[1]), axis=0)


def partner(u):
    lane = lax.broadcasted_iota(jnp.int32, u.shape, 1)
    small = jnp.where(lane < 8, pltpu.roll(u, HD - 8, 1), pltpu.roll(u, 8, 1))
    first = ((lane >= 16) & (lane < 44)) | ((lane >= 72) & (lane < 100))
    large = jnp.where(first, pltpu.roll(u, HD - 28, 1), pltpu.roll(u, 28, 1))
    return jnp.where(lane < 16, small, large)


def inverse_rms(u):
    return lax.rsqrt(jnp.mean(u * u, axis=-1, keepdims=True) + EPSILON)


class Names:
    pass


def kernel(S, G, names, *refs):
    n = Names()
    for name, ref in zip(names, refs):
        setattr(n, name, ref)
    n.orecv = (n.orecv0, n.orecv1)
    L = HEADS // G
    LT = L // 2
    R = n.q.shape[0]
    N = R * G
    TD = n.qt.shape[0]
    TS = TD * G
    Z = S // 2
    s = lax.axis_index("slab")
    x = lax.axis_index("heads")
    zi = s // 2
    ci = lax.rem(s, 2)
    sib = s + 1 - 2 * ci

    def xdev(d):
        return lax.rem(x + d, G)

    def sdev(d):
        return lax.rem(s + d, S)

    def zdev(d):
        return lax.rem(zi + d, Z) * 2 + ci

    def copy(src, dst, ss, rs, dev):
        return pltpu.make_async_remote_copy(
            src_ref=src, dst_ref=dst, send_sem=ss, recv_sem=rs, device_id=dev, device_id_type=MESH
        )

    bar = pltpu.get_barrier_semaphore()
    for d in range(1, G):
        pl.semaphore_signal(bar, inc=1, device_id={"heads": xdev(d)}, device_id_type=MESH)
    for d in range(1, S):
        pl.semaphore_signal(bar, inc=1, device_id={"slab": sdev(d)}, device_id_type=MESH)

    def tx(d):
        return copy(
            n.tsend.at[d], n.tg.at[s, x], n.tx_s.at[d], n.tx_r.at[d], {"heads": xdev(d)}
        )

    def tx_in(d):
        src = lax.rem(x + G - d, G)
        return copy(n.tsend.at[d], n.tg.at[s, src], n.tx_s.at[d], n.tx_r.at[d], {"heads": src})

    def tgat(sem, slab, dev):
        return copy(n.tg.at[slab], n.tg.at[slab], n.tg_s.at[sem], n.tg_r.at[slab], {"slab": dev})

    def inp(i, d):
        return copy(
            n.send.at[i, d],
            n.recv.at[i, :, pl.ds(pl.multiple_of(x * R, R), R), :],
            n.in_s.at[i, d],
            n.in_r.at[i, d],
            {"heads": xdev(d)},
        )

    def inp_in(i, d):
        src = lax.rem(x + G - d, G)
        return copy(
            n.send.at[i, d],
            n.recv.at[i, :, pl.ds(pl.multiple_of(src * R, R), R), :],
            n.in_s.at[i, d],
            n.in_r.at[i, d],
            {"heads": src},
        )

    def halo(i, up):
        return copy(
            n.recv.at[i, pl.ds(1, 2)],
            n.halo.at[i, 0 if up else 1],
            n.ha_s.at[i, 1 if up else 0],
            n.ha_r.at[i, 0 if up else 1],
            {"slab": s + 1 if up else s - 1},
        )

    def halo_in(i, below):
        k = 0 if below else 1
        return copy(
            n.recv.at[i, pl.ds(1, 2)],
            n.halo.at[i, k],
            n.ha_s.at[i, k],
            n.ha_r.at[i, k],
            {"slab": s - 1 if below else s + 1},
        )

    def hgrad(i, up):
        k = 1 if up else 0
        return copy(
            n.hsend.at[i, k],
            n.hrecv.at[i, 1 - k],
            n.hg_s.at[i, k],
            n.hg_r.at[i, 1 - k],
            {"slab": s + 1 if up else s - 1},
        )

    def hgrad_in(i, below):
        k = 0 if below else 1
        return copy(
            n.hsend.at[i, k],
            n.hrecv.at[i, k],
            n.hg_s.at[i, k],
            n.hg_r.at[i, k],
            {"slab": s - 1 if below else s + 1},
        )

    def outp(a, i, d):
        j = xdev(d)
        return copy(
            n.osend.at[a, i, j],
            n.orecv[a].at[x * L + i],
            n.o_s.at[a, i, d],
            n.o_r.at[a, i, d],
            {"heads": j},
        )

    def outp_in(a, i, d):
        src = lax.rem(x + G - d, G)
        return copy(
            n.osend.at[a, i, src],
            n.orecv[a].at[src * L + i],
            n.o_s.at[a, i, d],
            n.o_r.at[a, i, d],
            {"heads": src},
        )

    def stat(d):
        return copy(n.stats.at[s], n.stats.at[s], n.st_s.at[d], n.st_r.at[d], {"slab": sdev(d)})

    def stat_in(d):
        src = lax.rem(s + S - d, S)
        return copy(n.stats.at[src], n.stats.at[src], n.st_s.at[d], n.st_r.at[d], {"slab": src})

    def pair(z):
        return copy(
            n.tpart.at[2 * z + 1 - ci], n.tsib.at[z], n.p_s.at[z], n.p_r.at[z], {"slab": sib}
        )

    def zred(d):
        return copy(
            n.tz.at[lax.rem(zi + d, Z)], n.tzr.at[d], n.z_s.at[d], n.z_r.at[d], {"slab": zdev(d)}
        )

    def tfin(d):
        return copy(
            n.tfs.at[xdev(d)],
            n.tfr.at[pl.ds(x * L, L)],
            n.tf_s.at[d],
            n.tf_r.at[d],
            {"heads": xdev(d)},
        )

    def tfin_in(d):
        src = lax.rem(x + G - d, G)
        return copy(
            n.tfs.at[src], n.tfr.at[pl.ds(src * L, L)], n.tf_s.at[d], n.tf_r.at[d], {"heads": src}
        )

    def gainx(d):
        return copy(n.gx.at[0], n.gx.at[d], n.gx_s.at[d], n.gx_r.at[d], {"heads": xdev(d)})

    def gains(d):
        return copy(n.gs.at[0], n.gs.at[d], n.gs_s.at[d], n.gs_r.at[d], {"slab": sdev(d)})

    def lanes(h):
        return pl.ds(pl.multiple_of(h * HD, HD), HD)

    def by_head(h, carry):
        for a, ref in enumerate((n.q, n.k, n.v, n.g)):
            n.raw[h, a] = ref[:, lanes(h)]
        for a, ref in enumerate((n.qt, n.kt, n.vt, n.gt)):
            n.rawt[h, a] = ref[:, lanes(h)].astype(F32)
        return carry

    lax.fori_loop(0, HEADS, by_head, 0)

    def text_pre(i, carry):
        for d in range(G):
            h = n.order[xdev(d) * L + i]
            uq = n.rawt[h, 0]
            uk = n.rawt[h, 1]
            a = jnp.concatenate(
                [uq * inverse_rms(uq) * n.gqt[...], uk * inverse_rms(uk) * n.gkt[...]], axis=0
            ).astype(BF16)
            b = jnp.concatenate([n.rawt[h, 2], n.rawt[h, 3]], axis=0).astype(BF16)
            if d == 0:
                n.tg[s, x, i, 0] = a
                n.tg[s, x, i, 1] = b
            else:
                n.tsend[d, i, 0] = a
                n.tsend[d, i, 1] = b
        return carry

    lax.fori_loop(0, L, text_pre, 0)
    pl.semaphore_wait(bar, G - 1 + S - 1)
    for d in range(1, G):
        tx(d).start()

    def normed(u, gain):
        u = u.astype(F32)
        y = u * inverse_rms(u) * gain
        return (y * n.cos[...] + partner(y) * n.sin[...]).astype(BF16)

    def video_pre(i, carry):
        for d in range(G):
            h = n.order[xdev(d) * L + i]
            rows = (
                normed(n.raw[h, 0], n.gqv[...]),
                normed(n.raw[h, 1], n.gkv[...]),
                n.raw[h, 2],
                n.raw[h, 3],
            )
            for a in range(4):
                if d == 0:
                    n.recv[i, a, pl.ds(pl.multiple_of(x * R, R), R), :] = rows[a]
                else:
                    n.send[i, d, a] = rows[a]
            if d:
                inp(i, d).start()
        return carry

    lax.fori_loop(0, 1, video_pre, 0)
    for d in range(1, G):
        tx_in(d).wait_recv()
    tgat(0, s, sib).start()
    for d in range(1, Z):
        tgat(d, s, zdev(d)).start()
    lax.fori_loop(1, L, video_pre, 0)

    row = lax.broadcasted_iota(jnp.int32, (N, HD), 0)
    lane = lax.broadcasted_iota(jnp.int32, (N, HD), 1)
    tile_row = row // (N // 2)
    tile_col = lax.rem(row, GRID_W) // 8
    n.qaug[:, HD:] = jnp.where(lane == tile_row * 4 + tile_col, 1.0, 0.0).astype(BF16)

    def forward_halo(i):
        for d in range(1, G):
            inp_in(i, d).wait_recv()

        @pl.when(s < S - 1)
        def _():
            halo(i, True).start()

        @pl.when(s > 0)
        def _():
            halo(i, False).start()

    forward_halo(0)
    for d in range(1, Z):
        src = zdev(d)
        tgat(Z + d, src, sib).wait_recv()
        tgat(Z + d, src, sib).start()
    forward_halo(1)
    tgat(0, sib, sib).wait_recv()
    for d in range(1, Z):
        other = lax.rem(zi + d, Z) * 2 + 1 - ci
        tgat(Z + d, other, sib).wait_recv()

    def text_take(i, carry):
        for p in range(2):
            both = n.tg[:, :, i, p].astype(F32).reshape(S * G, 2 * TD, HD)
            for k in range(2):
                n.text[i, 2 * p + k] = (
                    both[:, k * TD : (k + 1) * TD].reshape(TEXT, HD).astype(BF16)
                )
        return carry

    lax.fori_loop(0, L, text_take, 0)

    def key_rows(at, count, k_rows, v_rows, feature):
        n.kaug[at : at + count, :HD] = k_rows
        n.kaug[at : at + count, HD:] = feature
        n.vbuf[at : at + count, :] = v_rows

    def attend(i, chunks):
        reach_y = n.reach[2 * (x * L + i)]
        reach_x = n.reach[2 * (x * L + i) + 1]
        fits = (jnp.abs(tile_row - lane // 4) <= reach_y) & (
            jnp.abs(tile_col - lax.rem(lane, 4)) <= reach_x
        )
        feature = jnp.where(fits, 0.0, NEGATIVE).astype(BF16)
        n.qaug[:, :HD] = n.recv[i, 0]
        key_rows(0, N, n.recv[i, 1], n.recv[i, 2], feature)
        key_rows(N, TEXT, n.text[i, 1], n.text[i, 2], n.tbias[...])
        if chunks > 3:
            for k, below in ((0, True), (1, False)):
                at = N + TEXT + k * N
                here = (s > 0) if below else (s < S - 1)

                @pl.when(here)
                def _():
                    halo_in(i, below).wait_recv()
                    key_rows(at, N, n.halo[i, k, 0], n.halo[i, k, 1], feature)

                @pl.when(jnp.logical_not(here))
                def _():
                    zero = jnp.zeros((N, HD), BF16)
                    key_rows(at, N, zero, zero, jnp.full((N, HD), NEGATIVE, BF16))

        for c in range(chunks):
            at = slice(c * 256, (c + 1) * 256)
            n.kT[:, at] = n.kaug[at, :HD].T
            n.vT[:, at] = n.vbuf[at, :].T

        def block(b, carry):
            at_q = pl.ds(pl.multiple_of(b * 256, 256), 256)
            qa = n.qaug[at_q, :]
            qn = n.qaug[at_q, :HD]
            gb = n.recv[i, 3, at_q, :]
            top = jnp.full((8, 256), NEGATIVE, F32)
            for c in range(chunks):
                at = slice(c * 256, (c + 1) * 256)
                sc = nt(n.kaug[at, :], qa)
                n.sbuf[at, :] = sc
                top = jnp.maximum(top, fold(sc, jnp.max))
            top = jnp.max(top, axis=0, keepdims=True) * SHARP
            total = jnp.zeros((8, 256), F32)
            acc = jnp.zeros((HD, 256), F32)
            for c in range(chunks):
                at = slice(c * 256, (c + 1) * 256)
                e = jnp.exp2(n.sbuf[at, :] * SHARP - top)
                n.sbuf[at, :] = e
                total = total + fold(e, jnp.sum)
                w = e.astype(BF16)
                acc = acc + nn(n.vT[:, at], w)
                dv = nn(w, gb)
                if c * 256 < N:
                    n.dvm[i, at, :] += dv
                elif c * 256 < N + TEXT:
                    n.dvt[i, :, :] += dv
                else:
                    n.dvh[c * 256 - N - TEXT : (c + 1) * 256 - N - TEXT, :] += dv
            inv = 1.0 / jnp.sum(total, axis=0, keepdims=True)
            out = (acc * inv).astype(BF16)
            gT = gb.astype(F32).T
            dot = jnp.sum(fold(gT * out.astype(F32), jnp.sum), axis=0, keepdims=True)
            dq = jnp.zeros((HD, 256), F32)
            for c in range(chunks):
                at = slice(c * 256, (c + 1) * 256)
                dp = nt(n.vbuf[at, :], gb)
                ds = ((n.sbuf[at, :] * inv) * (dp - dot)).astype(BF16)
                dq = dq + nn(n.kT[:, at], ds)
                dk = nn(ds, qn)
                if c * 256 < N:
                    n.dkm[i, at, :] += dk
                elif c * 256 < N + TEXT:
                    n.dkt[i, :, :] += dk
                else:
                    n.dkh[c * 256 - N - TEXT : (c + 1) * 256 - N - TEXT, :] += dk
            out = out.astype(F32).T.astype(BF16)
            dq = (dq * FACTOR).T.astype(BF16)
            for j in range(256 // R):
                n.osend[0, i, b * (256 // R) + j, 0] = out[j * R : (j + 1) * R]
                n.osend[0, i, b * (256 // R) + j, 1] = dq[j * R : (j + 1) * R]
            return carry

        n.dvm[i] = jnp.zeros((N, HD), F32)
        n.dkm[i] = jnp.zeros((N, HD), F32)
        n.dvt[i] = jnp.zeros((TEXT, HD), F32)
        n.dkt[i] = jnp.zeros((TEXT, HD), F32)
        if chunks > 3:
            n.dvh[...] = jnp.zeros((2 * N, HD), F32)
            n.dkh[...] = jnp.zeros((2 * N, HD), F32)
        lax.fori_loop(0, N // 256, block, 0)

        for d in range(1, G):
            outp(0, i, d).start()
        n.orecv[0][x * L + i] = n.osend[0, i, x]
        if chunks > 3:
            for k in range(2):
                n.hsend[i, k, 0] = (n.dkh[k * N : (k + 1) * N, :] * FACTOR).astype(BF16)
                n.hsend[i, k, 1] = n.dvh[k * N : (k + 1) * N, :].astype(BF16)

            @pl.when(s < S - 1)
            def _():
                hgrad(i, True).start()

            @pl.when(s > 0)
            def _():
                hgrad(i, False).start()

    def attend_wide(i, carry):
        attend(i, (3 * N + TEXT) // 256)
        return carry

    def attend_flat(i, carry):
        attend(i, (N + TEXT) // 256)
        return carry

    share = pl.ds(pl.multiple_of(s * TS, TS), TS)
    share_bias = n.tbias[share, :].astype(F32)
    share_bias = jnp.concatenate([share_bias, share_bias], axis=1)

    def text_scores(i):
        sv = nt(n.recv[i, 1], n.text[i, 0])
        st = nt(n.text[i, 1, share, :], n.text[i, 0]) + share_bias
        pv = nt(n.recv[i, 2], n.text[i, 3])
        pt = nt(n.text[i, 2, share, :], n.text[i, 3])
        return sv, st, pv, pt

    def text_first(i, carry):
        sv, st, pv, pt = text_scores(i)
        top = jnp.maximum(fold(sv, jnp.max), fold(st, jnp.max))
        top = jnp.max(top, axis=0, keepdims=True)
        ev = jnp.exp2((sv - top) * SHARP)
        et = jnp.exp2((st - top) * SHARP)
        total = fold(ev, jnp.sum) + fold(et, jnp.sum)
        dot = fold(ev * pv, jnp.sum) + fold(et * pt, jnp.sum)
        n.stats[s, 0, pl.ds(i, 1), :] = top
        n.stats[s, 1, pl.ds(i, 1), :] = jnp.sum(total, axis=0, keepdims=True)
        n.stats[s, 2, pl.ds(i, 1), :] = jnp.sum(dot, axis=0, keepdims=True)
        return carry

    def text_second(i, carry):
        sv, st, pv, pt = text_scores(i)
        tops = [n.stats[k, 0, pl.ds(i, 1), :] for k in range(S)]
        top = functools.reduce(jnp.maximum, tops)
        total = jnp.zeros((1, TEXT), F32)
        dot = jnp.zeros((1, TEXT), F32)
        for k in range(S):
            scale = jnp.exp2((tops[k] - top) * SHARP)
            total = total + n.stats[k, 1, pl.ds(i, 1), :] * scale
            dot = dot + n.stats[k, 2, pl.ds(i, 1), :] * scale
        inv = 1.0 / total
        dot = dot * inv
        ev = jnp.exp2((sv - top) * SHARP)
        et = jnp.exp2((st - top) * SHARP)
        wv = ev.astype(BF16)
        wt = et.astype(BF16)
        dsv = (ev * inv * (pv - dot)).astype(BF16)
        dst = (et * inv * (pt - dot)).astype(BF16)
        qt_ = n.text[i, 0]
        gt_ = n.text[i, 3]
        n.dvm[i] += nn(wv, gt_)
        n.dkm[i] += nn(dsv, qt_)
        n.dvt[i, share, :] += nn(wt, gt_)
        n.dkt[i, share, :] += nn(dst, qt_)
        kt_ = n.recv[i, 1].T
        vt_ = n.recv[i, 2].T
        ktt = n.text[i, 1, share, :].astype(F32).T.astype(BF16)
        vtt = n.text[i, 2, share, :].astype(F32).T.astype(BF16)
        out = (nn(vt_, wv) + nn(vtt, wt)) * inv
        dq = (nn(kt_, dsv) + nn(ktt, dst)) * FACTOR
        n.tpart[:, 0, i] = out.T.astype(BF16).reshape(S, TS, HD)
        n.tpart[:, 1, i] = dq.T.astype(BF16).reshape(S, TS, HD)
        n.tpart[:, 2, i] = (n.dkt[i] * FACTOR).astype(BF16).reshape(S, TS, HD)
        n.tpart[:, 3, i] = n.dvt[i].astype(BF16).reshape(S, TS, HD)
        return carry

    lax.fori_loop(0, 1, attend_wide, 0)
    forward_halo(2)
    lax.fori_loop(1, LT, attend_wide, 0)
    for i in range(LT, L):
        for d in range(1, G):
            inp_in(i, d).wait_recv()
    n.stats[s] = jnp.zeros((3, 8, TEXT), F32)
    lax.fori_loop(0, L, text_first, 0)
    for d in range(1, S):
        stat(d).start()
    lax.fori_loop(LT, L, attend_flat, 0)
    for d in range(1, S):
        stat_in(d).wait_recv()
    lax.fori_loop(0, L, text_second, 0)
    for z in range(Z):
        pair(z).start()

    def finish(i, wide):
        def pack(dk, dv):
            for j in range(G):
                n.osend[1, i, j, 0] = dk[j * R : (j + 1) * R].astype(BF16)
                n.osend[1, i, j, 1] = dv[j * R : (j + 1) * R].astype(BF16)

        if wide:
            for k, below in ((0, True), (1, False)):

                @pl.when((s > 0) if below else (s < S - 1))
                def _():
                    hgrad_in(i, below).wait_recv()
                    n.dkm[i] += n.hrecv[i, k, 0].astype(F32) * (1.0 / FACTOR)
                    n.dvm[i] += n.hrecv[i, k, 1].astype(F32)

        pack(n.dkm[i] * FACTOR, n.dvm[i])
        for d in range(1, G):
            outp(1, i, d).start()
        n.orecv[1][x * L + i] = n.osend[1, i, x]

    def finish_flat(i, carry):
        finish(i, False)
        return carry

    def finish_wide(i, carry):
        finish(i, True)
        return carry

    lax.fori_loop(LT, L, finish_flat, 0)
    for z in range(Z):
        pair(z).wait_recv()
        n.tz[z] = (n.tpart[2 * z + ci].astype(F32) + n.tsib[z].astype(F32)).astype(BF16)
    for d in range(1, Z):
        zred(d).start()
    lax.fori_loop(0, LT, finish_wide, 0)

    for i in range(L):
        for d in range(1, G):
            outp_in(0, i, d).wait_recv()

    def norm_back(u, dy, gain):
        r = inverse_rms(u)
        unit = u * r
        y = dy * gain
        grad = r * (y - unit * jnp.mean(y * unit, axis=-1, keepdims=True))
        return grad.astype(BF16), dy * unit

    def unrotate(y):
        return y * n.cos[...] - partner(y) * n.sin[...]

    def post_q(h, carry):
        p = n.place[h]
        n.o_out[:, lanes(h)] = n.orecv[0][p, 0]
        dy = unrotate(n.orecv[0][p, 1].astype(F32))
        grad, part = norm_back(n.q[:, lanes(h)].astype(F32), dy, n.gqv[...])
        n.o_dq[:, lanes(h)] = grad
        return carry + fold(part, jnp.sum)

    zero = jnp.zeros((8, HD), F32)
    gain_qv = lax.fori_loop(0, HEADS, post_q, zero)

    for d in range(1, Z):
        zred(d).wait_recv()
    summed = n.tz[zi].astype(F32)
    for d in range(1, Z):
        summed = summed + n.tzr[d].astype(F32)
    for j in range(G):
        rows = slice(j * TD, (j + 1) * TD)
        for p in range(2):
            n.tfs[j, :, p] = jnp.concatenate(
                [summed[2 * p, :, rows], summed[2 * p + 1, :, rows]], axis=1
            ).astype(BF16)
    for d in range(1, G):
        tfin(d).start()
    n.tfr[pl.ds(x * L, L)] = n.tfs[x]

    for i in range(L):
        for d in range(1, G):
            outp_in(1, i, d).wait_recv()

    def post_k(h, carry):
        p = n.place[h]
        n.o_dv[:, lanes(h)] = n.orecv[1][p, 1]
        dy = unrotate(n.orecv[1][p, 0].astype(F32))
        grad, part = norm_back(n.k[:, lanes(h)].astype(F32), dy, n.gkv[...])
        n.o_dk[:, lanes(h)] = grad
        return carry + fold(part, jnp.sum)

    gain_kv = lax.fori_loop(0, HEADS, post_k, zero)

    for d in range(1, G):
        tfin_in(d).wait_recv()

    def post_t(h, carry):
        p = n.place[h]
        a = n.tfr[p, 0].astype(F32)
        b = n.tfr[p, 1].astype(F32)
        n.o_outt[:, lanes(h)] = a[:TD].astype(BF16)
        n.o_dvt[:, lanes(h)] = b[TD:].astype(BF16)
        grad, part_q = norm_back(n.qt[:, lanes(h)].astype(F32), a[TD:], n.gqt[...])
        n.o_dqt[:, lanes(h)] = grad
        grad, part_k = norm_back(n.kt[:, lanes(h)].astype(F32), b[:TD], n.gkt[...])
        n.o_dkt[:, lanes(h)] = grad
        return carry[0] + fold(part_q, jnp.sum), carry[1] + fold(part_k, jnp.sum)

    gain_qt, gain_kt = lax.fori_loop(0, HEADS, post_t, (zero, zero))

    parts = [
        jnp.sum(part, axis=0, keepdims=True) for part in (gain_qv, gain_kv, gain_qt, gain_kt)
    ]
    n.gx[0] = jnp.concatenate(parts + [jnp.zeros((4, HD), F32)], axis=0)
    for d in range(1, G):
        gainx(d).start()
    for d in range(1, G):
        gainx(d).wait_recv()
    n.gs[0] = functools.reduce(lambda a, b: a + b, [n.gx[d] for d in range(G)])
    for d in range(1, S):
        gains(d).start()
    for d in range(1, S):
        gains(d).wait_recv()
    gain = functools.reduce(lambda a, b: a + b, [n.gs[d] for d in range(S)])
    n.o_gqv[...] = gain[0:1]
    n.o_gkv[...] = gain[1:2]
    n.o_gqt[...] = gain[2:3]
    n.o_gkt[...] = gain[3:4]

    for d in range(1, G):
        tx(d).wait_send()
        tfin(d).wait_send()
        gainx(d).wait_send()
        for i in range(L):
            inp(i, d).wait_send()
            outp(0, i, d).wait_send()
            outp(1, i, d).wait_send()
    tgat(0, s, sib).wait_send()
    for d in range(1, Z):
        tgat(d, s, zdev(d)).wait_send()
        tgat(Z + d, zdev(d), sib).wait_send()
        zred(d).wait_send()
    for z in range(Z):
        pair(z).wait_send()
    for d in range(1, S):
        stat(d).wait_send()
        gains(d).wait_send()
    for i in range(LT):
        for up in (True, False):

            @pl.when((s < S - 1) if up else (s > 0))
            def _():
                halo(i, up).wait_send()
                hgrad(i, up).wait_send()


def body(S, G, *args):
    (q, k, v, g, qt, kt, vt, gt, gqv, gkv, gqt, gkt, windows, text_mask) = args
    slab = lax.axis_index("slab")
    group = lax.axis_index("heads")
    R = q.shape[0]
    TD = qt.shape[0]
    TS = TD * G
    N = R * G
    L = HEADS // G
    LT = L // 2
    Z = S // 2
    order, place, reach = head_order(windows, G)
    index = (slab * G + group) * R + jnp.arange(R, dtype=jnp.int32)
    cos, sin = rope_tables(index, HD)
    tbias = jnp.broadcast_to(
        jnp.where(text_mask == 1, 0.0, NEGATIVE).astype(BF16)[:, None], (TEXT, HD)
    )
    smem = pl.BlockSpec(memory_space=pltpu.SMEM)
    vmem = pl.BlockSpec(memory_space=pltpu.VMEM)
    operands = [
        ("order", order, smem),
        ("place", place, smem),
        ("reach", reach, smem),
        ("cos", cos, vmem),
        ("sin", sin, vmem),
        ("tbias", tbias, vmem),
        ("gqv", gqv.reshape(1, HD), vmem),
        ("gkv", gkv.reshape(1, HD), vmem),
        ("gqt", gqt.reshape(1, HD), vmem),
        ("gkt", gkt.reshape(1, HD), vmem),
        ("q", q, vmem),
        ("k", k, vmem),
        ("v", v, vmem),
        ("g", g, vmem),
        ("qt", qt, vmem),
        ("kt", kt, vmem),
        ("vt", vt, vmem),
        ("gt", gt, vmem),
    ]
    rows = jax.ShapeDtypeStruct((R, D), BF16)
    trows = jax.ShapeDtypeStruct((TD, D), BF16)
    gain = jax.ShapeDtypeStruct((1, HD), F32)
    outs = [
        ("o_out", rows),
        ("o_outt", trows),
        ("o_dq", rows),
        ("o_dk", rows),
        ("o_dv", rows),
        ("o_dqt", trows),
        ("o_dkt", trows),
        ("o_dvt", trows),
        ("o_gqv", gain),
        ("o_gkv", gain),
        ("o_gqt", gain),
        ("o_gkt", gain),
    ]
    V = pltpu.VMEM
    dma = pltpu.SemaphoreType.DMA
    K = 3 * N + TEXT
    scratch = [
        ("raw", V((HEADS, 4, R, HD), BF16)),
        ("rawt", V((HEADS, 4, TD, HD), F32)),
        ("tsend", V((G, L, 2, 2 * TD, HD), BF16)),
        ("tg", V((S, G, L, 2, 2 * TD, HD), BF16)),
        ("text", V((L, 4, TEXT, HD), BF16)),
        ("send", V((L, G, 4, R, HD), BF16)),
        ("recv", V((L, 4, N, HD), BF16)),
        ("halo", V((LT, 2, 2, N, HD), BF16)),
        ("hsend", V((LT, 2, 2, N, HD), BF16)),
        ("hrecv", V((LT, 2, 2, N, HD), BF16)),
        ("osend", V((2, L, G, 2, R, HD), BF16)),
        ("orecv0", V((HEADS, 2, R, HD), BF16)),
        ("orecv1", V((HEADS, 2, R, HD), BF16)),
        ("stats", V((S, 3, 8, TEXT), F32)),
        ("tpart", V((S, 4, L, TS, HD), BF16)),
        ("tsib", V((Z, 4, L, TS, HD), BF16)),
        ("tz", V((Z, 4, L, TS, HD), BF16)),
        ("tzr", V((Z, 4, L, TS, HD), BF16)),
        ("tfs", V((G, L, 2, 2 * TD, HD), BF16)),
        ("tfr", V((HEADS, 2, 2 * TD, HD), BF16)),
        ("gx", V((G, 8, HD), F32)),
        ("gs", V((S, 8, HD), F32)),
        ("qaug", V((N, 2 * HD), BF16)),
        ("kaug", V((K, 2 * HD), BF16)),
        ("vbuf", V((K, HD), BF16)),
        ("kT", V((HD, K), BF16)),
        ("vT", V((HD, K), BF16)),
        ("sbuf", V((K, 256), F32)),
        ("dvm", V((L, N, HD), F32)),
        ("dkm", V((L, N, HD), F32)),
        ("dvt", V((L, TEXT, HD), F32)),
        ("dkt", V((L, TEXT, HD), F32)),
        ("dvh", V((2 * N, HD), F32)),
        ("dkh", V((2 * N, HD), F32)),
        ("tx_s", dma((G,))),
        ("tx_r", dma((G,))),
        ("tg_s", dma((2 * Z,))),
        ("tg_r", dma((S,))),
        ("in_s", dma((L, G))),
        ("in_r", dma((L, G))),
        ("ha_s", dma((LT, 2))),
        ("ha_r", dma((LT, 2))),
        ("hg_s", dma((LT, 2))),
        ("hg_r", dma((LT, 2))),
        ("o_s", dma((2, L, G))),
        ("o_r", dma((2, L, G))),
        ("st_s", dma((S,))),
        ("st_r", dma((S,))),
        ("p_s", dma((Z,))),
        ("p_r", dma((Z,))),
        ("z_s", dma((Z,))),
        ("z_r", dma((Z,))),
        ("tf_s", dma((G,))),
        ("tf_r", dma((G,))),
        ("gx_s", dma((G,))),
        ("gx_r", dma((G,))),
        ("gs_s", dma((S,))),
        ("gs_r", dma((S,))),
    ]
    names = [o[0] for o in operands] + [o[0] for o in outs] + [o[0] for o in scratch]
    result = pl.pallas_call(
        functools.partial(kernel, S, G, names),
        out_shape=[o[1] for o in outs],
        in_specs=[o[2] for o in operands],
        out_specs=[vmem] * len(outs),
        scratch_shapes=[o[1] for o in scratch],
        compiler_params=pltpu.CompilerParams(
            collective_id=0, has_side_effects=True, vmem_limit_bytes=60 << 20
        ),
        cost_estimate=pl.CostEstimate(
            flops=7 * 10**9, bytes_accessed=7 * 10**6, transcendentals=5 * 10**6
        ),
    )(*[o[1] for o in operands])
    return tuple(result[:8]) + tuple(r.reshape(HD) for r in result[8:])


def solution(mesh):
    S = mesh.shape["slab"]
    G = mesh.shape["heads"]
    rows = P(("replica", "slab", "heads"), None)
    split = P("replica")
    return jax.shard_map(
        functools.partial(body, S, G),
        mesh=mesh,
        in_specs=(rows,) * 8 + (split,) * 4 + (P(), split),
        out_specs=(rows,) * 8 + (split,) * 4,
        check_vma=False,
    )
```

```python
import functools

import jax
import jax.numpy as jnp
from jax import lax
from jax.experimental import pallas as pl
from jax.experimental.pallas import tpu as pltpu
from jax.sharding import PartitionSpec as P

HEADS = 24
HD = 128
D = 3072
TEXT = 256
GRID_H = 16
GRID_W = 32

EPSILON = 1e-06
ROPE_BASE = 256.0
NEGATIVE = -1e30
MANY = 6
FACTOR = HD ** (-0.5)
LOG2E = 1.4426950408889634
SHARP = FACTOR * LOG2E
MESH = pl.DeviceIdType.MESH
F32 = jnp.float32
BF16 = jnp.bfloat16


def head_order(windows, groups):
    local = HEADS // groups
    wide = windows[:, 0] == 3
    ids = jnp.arange(HEADS, dtype=jnp.int32)
    before = ids[None, :] < ids[:, None]
    rank_wide = jnp.sum(before & wide[None, :], axis=1, dtype=jnp.int32)
    rank_flat = jnp.sum(before & ~wide[None, :], axis=1, dtype=jnp.int32)
    slot = jnp.where(wide, rank_wide // groups, local // 2 + rank_flat // groups)
    group = jnp.where(wide, rank_wide % groups, rank_flat % groups)
    place = group * local + slot
    code = ids + windows[:, 1] // 2 * 32 + windows[:, 2] // 2 * 64
    chosen = place[None, :] == ids[:, None]
    code = jnp.sum(jnp.where(chosen, code[None, :], 0), axis=1, dtype=jnp.int32)
    return code + place * 128


def nt(a, b):
    return lax.dot_general(a, b, (((1,), (1,)), ((), ())), preferred_element_type=F32)


def nn(a, b):
    return lax.dot_general(a, b, (((1,), (0,)), ((), ())), preferred_element_type=F32)


def fold(values, op):
    return op(values.reshape(values.shape[0] // 8, 8, values.shape[1]), axis=0)


def partner_lane(lane):
    first = ((lane >= 16) & (lane < 44)) | ((lane >= 72) & (lane < 100))
    small = jnp.where(lane < 8, lane + 8, lane - 8)
    return jnp.where(lane < 16, small, jnp.where(first, lane + 28, lane - 28))


def partner(u):
    lane = lax.broadcasted_iota(jnp.int32, u.shape, 1)
    first = ((lane >= 16) & (lane < 44)) | ((lane >= 72) & (lane < 100))
    small = jnp.where(lane < 8, pltpu.roll(u, HD - 8, 1), pltpu.roll(u, 8, 1))
    large = jnp.where(first, pltpu.roll(u, HD - 28, 1), pltpu.roll(u, 28, 1))
    return jnp.where(lane < 16, small, large)


def rope_tables(frame, first_row, rows):
    lane = lax.broadcasted_iota(jnp.int32, (rows, HD), 1)
    row = lax.broadcasted_iota(jnp.int32, (rows, HD), 0)
    short = lane < 16
    middle = lane < 72
    inside = jnp.where(short, lane, jnp.where(middle, lane - 16, lane - 72))
    half = jnp.where(short, 8, 28)
    offset = jnp.where(inside >= half, inside - half, inside)
    place = jnp.where(short, frame, jnp.where(middle, first_row + row // GRID_W, lax.rem(row, GRID_W)))
    rate = jnp.where(short, -1.0, -16.0 / 56.0)
    angle = place.astype(F32) * jnp.exp2(offset.astype(F32) * rate)
    sine = jnp.sin(angle)
    return jnp.cos(angle), jnp.where(inside < half, -sine, sine)


class Names:
    pass


def kernel(S, G, names, *refs):
    n = Names()
    for name, ref in zip(names, refs):
        setattr(n, name, ref)
    n.orecv = (n.orecv0, n.orecv1)
    L = HEADS // G
    LT = L // 2
    R = n.q.shape[0]
    N = R * G
    TD = n.qt.shape[0]
    TS = TD * G
    Z = S // 2
    s = lax.axis_index("slab")
    x = lax.axis_index("heads")
    zi = s // 2
    ci = lax.rem(s, 2)
    sib = s + 1 - 2 * ci

    def xdev(d):
        return lax.rem(x + d, G)

    def sdev(d):
        return lax.rem(s + d, S)

    def zdev(d):
        return lax.rem(zi + d, Z) * 2 + ci

    def copy(src, dst, ss, rs, dev):
        return pltpu.make_async_remote_copy(
            src_ref=src, dst_ref=dst, send_sem=ss, recv_sem=rs, device_id=dev, device_id_type=MESH
        )

    bar = pltpu.get_barrier_semaphore()
    for d in range(1, G):
        pl.semaphore_signal(bar, inc=1, device_id={"heads": xdev(d)}, device_id_type=MESH)
    for d in range(1, S):
        pl.semaphore_signal(bar, inc=1, device_id={"slab": sdev(d)}, device_id_type=MESH)

    tg = (n.tg0, n.tg1)

    def tx(p, d):
        return copy(
            n.tsend.at[p, d], tg[p].at[s, x], n.tx_s.at[p, d], n.tx_r.at[p, d], {"heads": xdev(d)}
        )

    def tx_in(p, d):
        src = lax.rem(x + G - d, G)
        return copy(
            n.tsend.at[p, d], tg[p].at[s, src], n.tx_s.at[p, d], n.tx_r.at[p, d], {"heads": src}
        )

    def tgat(p, sem, slab, dev):
        return copy(
            tg[p].at[slab], tg[p].at[slab], n.tg_s.at[p, sem], n.tg_r.at[p, slab], {"slab": dev}
        )

    def trelay(p, half, src, dev):
        rows = tg[p].at[src, pl.ds(half * (G // 2), G // 2)]
        return copy(rows, rows, n.tg_s.at[p, 3 + half], n.tg_r.at[p, S + half], {"slab": dev})

    def inp(i, d):
        return copy(
            n.send.at[i, d],
            n.recv.at[i, :, pl.ds(pl.multiple_of(x * R, R), R), :],
            n.in_s.at[i, d],
            n.in_r.at[i, d],
            {"heads": xdev(d)},
        )

    def inp_in(i, d):
        src = lax.rem(x + G - d, G)
        return copy(
            n.send.at[i, d],
            n.recv.at[i, :, pl.ds(pl.multiple_of(src * R, R), R), :],
            n.in_s.at[i, d],
            n.in_r.at[i, d],
            {"heads": src},
        )

    def halo(i, up):
        return copy(
            n.recv.at[i, pl.ds(1, 2)],
            n.halo.at[i, 0 if up else 1],
            n.ha_s.at[i, 1 if up else 0],
            n.ha_r.at[i, 0 if up else 1],
            {"slab": s + 1 if up else s - 1},
        )

    def halo_in(i, below):
        k = 0 if below else 1
        return copy(
            n.recv.at[i, pl.ds(1, 2)],
            n.halo.at[i, k],
            n.ha_s.at[i, k],
            n.ha_r.at[i, k],
            {"slab": s - 1 if below else s + 1},
        )

    def hgrad(i, up):
        k = 1 if up else 0
        return copy(
            n.hsend.at[i, k],
            n.hrecv.at[i, 1 - k],
            n.hg_s.at[i, k],
            n.hg_r.at[i, 1 - k],
            {"slab": s + 1 if up else s - 1},
        )

    def hgrad_in(i, below):
        k = 0 if below else 1
        return copy(
            n.hsend.at[i, k],
            n.hrecv.at[i, k],
            n.hg_s.at[i, k],
            n.hg_r.at[i, k],
            {"slab": s - 1 if below else s + 1},
        )

    def outp(a, i, d):
        j = xdev(d)
        return copy(
            n.osend.at[a, i, j],
            n.orecv[a].at[x * L + i],
            n.o_s.at[a, i, d],
            n.o_r.at[a, i, d],
            {"heads": j},
        )

    def outp_in(a, i, d):
        src = lax.rem(x + G - d, G)
        return copy(
            n.osend.at[a, i, src],
            n.orecv[a].at[src * L + i],
            n.o_s.at[a, i, d],
            n.o_r.at[a, i, d],
            {"heads": src},
        )

    def stat_pair():
        return copy(n.stats.at[0], n.stats.at[1], n.st_s.at[0], n.st_r.at[0], {"slab": sib})

    def stat(d):
        at = n.chips.at[zi]
        return copy(at, at, n.st_s.at[d], n.st_r.at[d], {"slab": zdev(d)})

    def stat_in(d):
        src = lax.rem(zi + Z - d, Z)
        at = n.chips.at[src]
        return copy(at, at, n.st_s.at[d], n.st_r.at[d], {"slab": src * 2 + ci})

    def pair(z):
        return copy(
            n.tpart.at[2 * z + 1 - ci], n.tsib.at[z], n.p_s.at[z], n.p_r.at[z], {"slab": sib}
        )

    def zred(k):
        up = k % 2 == 0
        to = lax.rem(zi + (1 if up else Z - 1), Z)
        low = k in (0, 3, 4)
        rows = pl.ds(0 if low else 2, 2)
        if k < 2:
            src, dst = n.tz.at[lax.rem(zi + 2, Z), rows], n.tzh.at[k]
        else:
            src, dst = n.tz.at[to, rows], n.tzr.at[k % 2, rows]
        return copy(src, dst, n.z_s.at[k], n.z_r.at[k], {"slab": to * 2 + ci})

    def tfin(d):
        return copy(
            n.tfs.at[xdev(d)],
            n.tfr.at[pl.ds(x * L, L)],
            n.tf_s.at[d],
            n.tf_r.at[d],
            {"heads": xdev(d)},
        )

    def tfin_in(d):
        src = lax.rem(x + G - d, G)
        return copy(
            n.tfs.at[src], n.tfr.at[pl.ds(src * L, L)], n.tf_s.at[d], n.tf_r.at[d], {"heads": src}
        )

    def gainx(d):
        return copy(n.gx.at[0], n.gx.at[d], n.gx_s.at[d], n.gx_r.at[d], {"heads": xdev(d)})

    def gains(d):
        return copy(n.gs.at[0], n.gs.at[d], n.gs_s.at[d], n.gs_r.at[d], {"slab": sdev(d)})

    def order(p):
        return n.table[p] & 31

    def place(h):
        return n.table[h] >> 7

    def lanes(h):
        return pl.ds(pl.multiple_of(h * HD, HD), HD)

    def by_head(h, carry):
        for a, ref in enumerate((n.q, n.k, n.v, n.g)):
            n.raw[h, a] = ref[:, lanes(h)]
        return carry

    for h in range(HEADS):
        for a, ref in enumerate((n.qt, n.kt, n.vt, n.gt)):
            n.rawt[a, h] = ref[:, h * HD : (h + 1) * HD].astype(F32)

    k_lane = lax.broadcasted_iota(jnp.int32, (HD, HD), 0)
    lane = lax.broadcasted_iota(jnp.int32, (HD, HD), 1)
    n.swap[...] = jnp.where(k_lane == partner_lane(lane), 1.0, 0.0).astype(BF16)
    n.mean[...] = jnp.full((2 * HD, HD), 1.0 / HD, BF16)
    bias = jnp.where(n.tmask[...] == 1, 0.0, NEGATIVE)
    n.tbias[...] = jnp.broadcast_to(bias, (HD, TEXT)).T.astype(BF16)

    def lane_mean(values):
        high = values.astype(BF16)
        low = (values - high.astype(F32)).astype(BF16)
        return nn(jnp.concatenate([high, low], axis=1), n.mean[...])

    def inverse_rms(u):
        return lax.rsqrt(lane_mean(u * u) + EPSILON)

    for a, gain in ((0, n.gqt), (1, n.gkt)):
        u = n.rawt[a].reshape(HEADS * TD, HD)
        n.normt[a] = (u * inverse_rms(u) * gain[...]).reshape(HEADS, TD, HD)

    def text_pre(i, carry):
        for d in range(G):
            h = order(xdev(d) * L + i)
            rows = (
                jnp.concatenate([n.normt[1, h], n.rawt[2, h]], axis=0).astype(BF16),
                jnp.concatenate([n.normt[0, h], n.rawt[3, h]], axis=0).astype(BF16),
            )
            for p in range(2):
                if d == 0:
                    tg[p][s, x, i] = rows[p]
                else:
                    n.tsend[p, d, i] = rows[p]
        return carry

    lax.fori_loop(0, L, text_pre, 0)
    pl.semaphore_wait(bar, G - 1 + S - 1)
    for p in range(2):
        for d in range(1, G):
            tx(p, d).start()
    lax.fori_loop(0, HEADS, by_head, 0)
    cos, sin = rope_tables(s, x * (R // GRID_W), R)
    n.cos[...] = cos
    n.sin[...] = sin
    for k, gain in ((0, n.gqv), (1, n.gkv)):
        n.gcos[k] = gain[...] * cos
        n.gsin[k] = partner(jnp.broadcast_to(gain[...], (8, HD)))[0:1] * sin
    def normed(u, k):
        f = u.astype(F32)
        y = f * n.gcos[k] + nn(u, n.swap[...]) * n.gsin[k]
        return (y * inverse_rms(f)).astype(BF16)

    def video_pre(i, carry):
        for d in range(G):
            h = order(xdev(d) * L + i)
            rows = (normed(n.raw[h, 0], 0), normed(n.raw[h, 1], 1), n.raw[h, 2], n.raw[h, 3])
            for a in range(4):
                if d == 0:
                    n.recv[i, a, pl.ds(pl.multiple_of(x * R, R), R), :] = rows[a]
                else:
                    n.send[i, d, a] = rows[a]
        return carry

    def send_slot(i):
        for d in range(1, G):
            inp(i, d).start()

    after, behind, across = zdev(1), zdev(Z - 1), zdev(2)

    def text_out(p):
        for d in range(1, G):
            tx_in(p, d).wait_recv()
        tgat(p, 1, s, after).start()
        tgat(p, 2, s, behind).start()
        tgat(p, 0, s, sib).start()

    def text_relay(p):
        tgat(p, 1, behind, behind).wait_recv()
        trelay(p, 0, behind, after).start()
        tgat(p, 5, behind, sib).start()
        tgat(p, 2, after, after).wait_recv()
        trelay(p, 1, after, behind).start()
        tgat(p, 6, after, sib).start()

    def text_forward(p):
        trelay(p, 0, across, behind).wait_recv()
        trelay(p, 1, across, after).wait_recv()
        tgat(p, 7, across, sib).start()

    def text_in(p):
        tgat(p, 0, sib, sib).wait_recv()
        for d in range(1, Z):
            other = lax.rem(zi + d, Z) * 2 + 1 - ci
            tgat(p, 0, other, sib).wait_recv()

        def text_take(i, carry):
            both = tg[p][:, :, i].astype(F32).reshape(S * G, 2 * TD, HD)
            for k in range(2):
                n.text[i, 2 * p + k] = (
                    both[:, k * TD : (k + 1) * TD].reshape(TEXT, HD).astype(BF16)
                )
            return carry

        lax.fori_loop(0, L, text_take, 0)

    lax.fori_loop(0, 1, video_pre, 0)
    send_slot(0)
    lax.fori_loop(1, 2, video_pre, 0)
    text_out(0)
    send_slot(1)
    lax.fori_loop(2, L, video_pre, 0)

    row = lax.broadcasted_iota(jnp.int32, (N, HD), 0)
    lane = lax.broadcasted_iota(jnp.int32, (N, HD), 1)
    tile_row = row // (N // 2)
    tile_col = lax.rem(row, GRID_W) // 8
    n.qaug[:, HD:] = jnp.where(lane == tile_row * 4 + tile_col, 1.0, 0.0).astype(BF16)

    def forward_halo(i):
        for d in range(1, G):
            inp_in(i, d).wait_recv()
        send_slot(i + 2)

        @pl.when(s < S - 1)
        def _():
            halo(i, True).start()

        @pl.when(s > 0)
        def _():
            halo(i, False).start()

    def key_rows(at, count, k_rows, v_rows, feature):
        n.kaug[at : at + count, :HD] = k_rows
        n.kaug[at : at + count, HD:] = feature
        n.vbuf[at : at + count, :] = v_rows

    def attend(i, chunks):
        reach_y = (n.table[x * L + i] >> 5) & 1
        reach_x = (n.table[x * L + i] >> 6) & 1
        fits = (jnp.abs(tile_row - lane // 4) <= reach_y) & (
            jnp.abs(tile_col - lax.rem(lane, 4)) <= reach_x
        )
        feature = jnp.where(fits, 0.0, NEGATIVE).astype(BF16)
        n.qaug[:, :HD] = n.recv[i, 0]
        key_rows(0, N, n.recv[i, 1], n.recv[i, 2], feature)
        key_rows(N, TEXT, n.text[i, 0], n.text[i, 1], n.tbias[...])
        if chunks > 3:
            for k, below in ((0, True), (1, False)):
                at = N + TEXT + k * N
                here = (s > 0) if below else (s < S - 1)

                @pl.when(here)
                def _():
                    halo_in(i, below).wait_recv()
                    key_rows(at, N, n.halo[i, k, 0], n.halo[i, k, 1], feature)

                @pl.when(jnp.logical_not(here))
                def _():
                    zero = jnp.zeros((N, HD), BF16)
                    key_rows(at, N, zero, zero, jnp.full((N, HD), NEGATIVE, BF16))

        for c in range(chunks):
            at = slice(c * 256, (c + 1) * 256)
            n.kT[:, at] = n.kaug[at, :HD].T
            n.vT[:, at] = n.vbuf[at, :].T

        def block(b, carry):
            at_q = pl.ds(pl.multiple_of(b * 256, 256), 256)
            qa = n.qaug[at_q, :]
            qn = n.qaug[at_q, :HD]
            gb = n.recv[i, 3, at_q, :]
            top = jnp.full((8, 256), NEGATIVE, F32)
            for c in range(chunks):
                at = slice(c * 256, (c + 1) * 256)
                sc = nt(n.kaug[at, :], qa)
                n.sbuf[at, :] = sc
                top = jnp.maximum(top, fold(sc, jnp.max))
            top = jnp.max(top, axis=0, keepdims=True) * SHARP
            total = jnp.zeros((8, 256), F32)
            acc = jnp.zeros((HD, 256), F32)
            for c in range(chunks):
                at = slice(c * 256, (c + 1) * 256)
                e = jnp.exp2(n.sbuf[at, :] * SHARP - top)
                n.sbuf[at, :] = e
                total = total + fold(e, jnp.sum)
                w = e.astype(BF16)
                acc = acc + nn(n.vT[:, at], w)
                dv = nn(w, gb)
                if c * 256 < N:
                    n.dvm[i, at, :] += dv
                elif c * 256 < N + TEXT:
                    n.dvt[i, :, :] += dv
                else:
                    n.dvh[c * 256 - N - TEXT : (c + 1) * 256 - N - TEXT, :] += dv
            inv = 1.0 / jnp.sum(total, axis=0, keepdims=True)
            out = (acc * inv).astype(BF16)
            gT = gb.astype(F32).T
            dot = jnp.sum(fold(gT * out.astype(F32), jnp.sum), axis=0, keepdims=True)
            dq = jnp.zeros((HD, 256), F32)
            for c in range(chunks):
                at = slice(c * 256, (c + 1) * 256)
                dp = nt(n.vbuf[at, :], gb)
                ds = ((n.sbuf[at, :] * inv) * (dp - dot)).astype(BF16)
                dq = dq + nn(n.kT[:, at], ds)
                dk = nn(ds, qn)
                if c * 256 < N:
                    n.dkm[i, at, :] += dk
                elif c * 256 < N + TEXT:
                    n.dkt[i, :, :] += dk
                else:
                    n.dkh[c * 256 - N - TEXT : (c + 1) * 256 - N - TEXT, :] += dk
            out = out.astype(F32).T.astype(BF16)
            dq = (dq * FACTOR).T.astype(BF16)
            for j in range(256 // R):
                n.osend[0, i, b * (256 // R) + j, 0] = out[j * R : (j + 1) * R]
                n.osend[0, i, b * (256 // R) + j, 1] = dq[j * R : (j + 1) * R]
            return carry

        n.dvm[i] = jnp.zeros((N, HD), F32)
        n.dkm[i] = jnp.zeros((N, HD), F32)
        n.dvt[i] = jnp.zeros((TEXT, HD), F32)
        n.dkt[i] = jnp.zeros((TEXT, HD), F32)
        if chunks > 3:
            n.dvh[...] = jnp.zeros((2 * N, HD), F32)
            n.dkh[...] = jnp.zeros((2 * N, HD), F32)
        lax.fori_loop(0, N // 256, block, 0)

        for d in range(1, G):
            outp(0, i, d).start()
        n.orecv[0][x * L + i] = n.osend[0, i, x]
        if chunks > 3:
            for k in range(2):
                n.hsend[i, k, 0] = (n.dkh[k * N : (k + 1) * N, :] * FACTOR).astype(BF16)
                n.hsend[i, k, 1] = n.dvh[k * N : (k + 1) * N, :].astype(BF16)

            @pl.when(s < S - 1)
            def _():
                hgrad(i, True).start()

            @pl.when(s > 0)
            def _():
                hgrad(i, False).start()

    share = pl.ds(pl.multiple_of(s * TS, TS), TS)
    share_bias = n.tbias[share, :].astype(F32)
    share_bias = jnp.concatenate([share_bias, share_bias], axis=1)

    def text_scores(i):
        sv = nt(n.recv[i, 1], n.text[i, 2])
        st = nt(n.text[i, 0, share, :], n.text[i, 2]) + share_bias
        pv = nt(n.recv[i, 2], n.text[i, 3])
        pt = nt(n.text[i, 1, share, :], n.text[i, 3])
        return sv, st, pv, pt

    def text_first(i, carry):
        sv, st, pv, pt = text_scores(i)
        top = jnp.maximum(fold(sv, jnp.max), fold(st, jnp.max))
        top = jnp.max(top, axis=0, keepdims=True)
        ev = jnp.exp2((sv - top) * SHARP)
        et = jnp.exp2((st - top) * SHARP)
        total = fold(ev, jnp.sum) + fold(et, jnp.sum)
        dot = fold(ev * pv, jnp.sum) + fold(et * pt, jnp.sum)
        n.stats[0, 0, pl.ds(i, 1), :] = top
        n.stats[0, 1, pl.ds(i, 1), :] = jnp.sum(total, axis=0, keepdims=True)
        n.stats[0, 2, pl.ds(i, 1), :] = jnp.sum(dot, axis=0, keepdims=True)
        return carry

    def text_second(i, carry):
        sv, st, pv, pt = text_scores(i)
        tops = [n.chips[k, 0, pl.ds(i, 1), :] for k in range(Z)]
        top = functools.reduce(jnp.maximum, tops)
        total = jnp.zeros((1, TEXT), F32)
        dot = jnp.zeros((1, TEXT), F32)
        for k in range(Z):
            scale = jnp.exp2((tops[k] - top) * SHARP)
            total = total + n.chips[k, 1, pl.ds(i, 1), :] * scale
            dot = dot + n.chips[k, 2, pl.ds(i, 1), :] * scale
        inv = 1.0 / total
        dot = dot * inv
        ev = jnp.exp2((sv - top) * SHARP)
        et = jnp.exp2((st - top) * SHARP)
        wv = ev.astype(BF16)
        wt = et.astype(BF16)
        dsv = (ev * inv * (pv - dot)).astype(BF16)
        dst = (et * inv * (pt - dot)).astype(BF16)
        qt_ = n.text[i, 2]
        gt_ = n.text[i, 3]
        n.dvm[i] += nn(wv, gt_)
        n.dkm[i] += nn(dsv, qt_)
        n.dvt[i, share, :] += nn(wt, gt_)
        n.dkt[i, share, :] += nn(dst, qt_)
        kt_ = n.recv[i, 1].T
        vt_ = n.recv[i, 2].T
        ktt = n.text[i, 0, share, :].astype(F32).T.astype(BF16)
        vtt = n.text[i, 1, share, :].astype(F32).T.astype(BF16)
        out = (nn(vt_, wv) + nn(vtt, wt)) * inv
        dq = (nn(kt_, dsv) + nn(ktt, dst)) * FACTOR
        n.tpart[:, 0, i] = out.T.astype(BF16).reshape(S, TS, HD)
        n.tpart[:, 1, i] = dq.T.astype(BF16).reshape(S, TS, HD)
        n.tpart[:, 2, i] = (n.dkt[i] * FACTOR).astype(BF16).reshape(S, TS, HD)
        n.tpart[:, 3, i] = n.dvt[i].astype(BF16).reshape(S, TS, HD)
        return carry

    forward_halo(0)
    text_relay(0)
    text_out(1)
    forward_halo(1)
    text_forward(0)
    forward_halo(2)
    text_relay(1)
    text_in(0)

    def slot_in(i):
        for d in range(1, G):
            inp_in(i, d).wait_recv()

    def attend_pair(i, carry):
        @pl.when(i == 1)
        def _():
            text_forward(1)

        @pl.when(i == LT - 1)
        def _():
            text_in(1)
            slot_in(L - 1)
            n.stats[0] = jnp.zeros((3, 8, TEXT), F32)
            lax.fori_loop(0, L, text_first, 0)
            stat_pair().start()

        attend(i, (3 * N + TEXT) // 256)

        @pl.when(i == LT - 1)
        def _():
            stat_pair().wait_recv()
            top = jnp.maximum(n.stats[0, 0], n.stats[1, 0])
            scales = [jnp.exp2((n.stats[k, 0] - top) * SHARP) for k in range(2)]
            n.chips[zi, 0] = top
            for a in (1, 2):
                n.chips[zi, a] = n.stats[0, a] * scales[0] + n.stats[1, a] * scales[1]
            for d in range(1, Z):
                stat(d).start()

        @pl.when(i < LT - 1)
        def _():
            slot_in(LT + i)

        @pl.when(i == 0)
        def _():
            send_slot(L - 1)

        attend(LT + i, (N + TEXT) // 256)
        return carry

    lax.fori_loop(0, LT, attend_pair, 0)
    for d in range(1, Z):
        stat_in(d).wait_recv()
    lax.fori_loop(0, L, text_second, 0)
    for z in range(Z):
        pair(z).start()

    def finish(i, wide):
        def pack(dk, dv):
            for j in range(G):
                n.osend[1, i, j, 0] = dk[j * R : (j + 1) * R].astype(BF16)
                n.osend[1, i, j, 1] = dv[j * R : (j + 1) * R].astype(BF16)

        if wide:
            for k, below in ((0, True), (1, False)):

                @pl.when((s > 0) if below else (s < S - 1))
                def _():
                    hgrad_in(i, below).wait_recv()
                    n.dkm[i] += n.hrecv[i, k, 0].astype(F32) * (1.0 / FACTOR)
                    n.dvm[i] += n.hrecv[i, k, 1].astype(F32)

        pack(n.dkm[i] * FACTOR, n.dvm[i])
        for d in range(1, G):
            outp(1, i, d).start()
        n.orecv[1][x * L + i] = n.osend[1, i, x]

    def finish_flat(i, carry):
        finish(i, False)
        return carry

    def finish_wide(i, carry):
        finish(i, True)
        return carry

    def relay_sums():
        for k in range(2):
            to = lax.rem(zi + (1 if k == 0 else Z - 1), Z)
            rows = slice(2 * k, 2 * k + 2)
            zred(k).wait_recv()
            n.tz[to, rows] = (n.tz[to, rows].astype(F32) + n.tzh[k].astype(F32)).astype(BF16)
            zred(4 + k).start()

    lax.fori_loop(LT, L, finish_flat, 0)
    for z in range(Z):
        pair(z).wait_recv()
        n.tz[z] = (n.tpart[2 * z + ci].astype(F32) + n.tsib[z].astype(F32)).astype(BF16)
    for k in range(4):
        zred(k).start()
    lax.fori_loop(0, LT - 1, finish_wide, 0)
    relay_sums()
    lax.fori_loop(LT - 1, LT, finish_wide, 0)

    for i in range(L):
        for d in range(1, G):
            outp_in(0, i, d).wait_recv()

    def norm_back(u, dy, gain):
        f = u.astype(F32)
        r = inverse_rms(f)
        unit = f * r
        part = dy * unit
        return r * (dy * gain - unit * lane_mean(part * gain)), part

    cos_many = jnp.concatenate([n.cos[...]] * MANY, axis=0)
    sin_many = jnp.concatenate([n.sin[...]] * MANY, axis=0)

    def post(step, carry, received, back, plain, source, gain, out_plain, out_grad):
        heads = [MANY * step + k for k in range(MANY)]
        places = [place(h) for h in heads]
        for h, p in zip(heads, places):
            out_plain[:, lanes(h)] = received[p, plain]
        y = jnp.concatenate([received[p, back] for p in places], axis=0)
        u = jnp.concatenate([source[:, lanes(h)] for h in heads], axis=0)
        dy = y.astype(F32) * cos_many - nn(y, n.swap[...]) * sin_many
        grad, part = norm_back(u, dy, gain[...])
        for k, h in enumerate(heads):
            out_grad[:, lanes(h)] = grad[k * R : (k + 1) * R].astype(BF16)
        return carry + fold(part, jnp.sum)

    def post_q(step, carry):
        return post(step, carry, n.orecv[0], 1, 0, n.q, n.gqv, n.o_out, n.o_dq)

    def post_k(step, carry):
        return post(step, carry, n.orecv[1], 0, 1, n.k, n.gkv, n.o_dv, n.o_dk)

    zero = jnp.zeros((8, HD), F32)
    gain_qv = lax.fori_loop(0, HEADS // MANY, post_q, zero)

    for k in range(2, 6):
        zred(k).wait_recv()
    summed = n.tz[zi].astype(F32) + n.tzr[0].astype(F32) + n.tzr[1].astype(F32)
    for j in range(G):
        rows = slice(j * TD, (j + 1) * TD)
        for p in range(2):
            n.tfs[j, :, p] = jnp.concatenate(
                [summed[2 * p, :, rows], summed[2 * p + 1, :, rows]], axis=1
            ).astype(BF16)
    for d in range(1, G):
        tfin(d).start()
    n.tfr[pl.ds(x * L, L)] = n.tfs[x]

    for i in range(L):
        for d in range(1, G):
            outp_in(1, i, d).wait_recv()

    gain_kv = lax.fori_loop(0, HEADS // MANY, post_k, zero)

    def text_order(p, carry):
        h = order(p)
        n.rawp[0, p] = n.rawt[0, h]
        n.rawp[1, p] = n.rawt[1, h]
        return carry

    lax.fori_loop(0, HEADS, text_order, 0)
    for d in range(1, G):
        tfin_in(d).wait_recv()

    first = n.tfr[:, 0].astype(F32)
    second = n.tfr[:, 1].astype(F32)
    n.tres[0] = first[:, :TD]
    n.tres[3] = second[:, TD:]
    gain_t = []
    for k, dy, gain in ((0, first[:, TD:], n.gqt), (1, second[:, :TD], n.gkt)):
        u = n.rawp[k].reshape(HEADS * TD, HD)
        grad, part = norm_back(u, dy.reshape(HEADS * TD, HD), gain[...])
        n.tres[1 + k] = grad.reshape(HEADS, TD, HD)
        gain_t.append(fold(part, jnp.sum))

    def post_t(h, carry):
        p = place(h)
        n.o_outt[:, lanes(h)] = n.tres[0, p].astype(BF16)
        n.o_dqt[:, lanes(h)] = n.tres[1, p].astype(BF16)
        n.o_dkt[:, lanes(h)] = n.tres[2, p].astype(BF16)
        n.o_dvt[:, lanes(h)] = n.tres[3, p].astype(BF16)
        return carry

    parts = [
        jnp.sum(part, axis=0, keepdims=True) for part in (gain_qv, gain_kv, *gain_t)
    ]
    n.gx[0] = jnp.concatenate(parts + [jnp.zeros((4, HD), F32)], axis=0)
    for d in range(1, G):
        gainx(d).start()
    lax.fori_loop(0, HEADS, post_t, 0)
    for d in range(1, G):
        gainx(d).wait_recv()
    n.gs[0] = functools.reduce(lambda a, b: a + b, [n.gx[d] for d in range(G)])
    for d in range(1, S):
        gains(d).start()
    for d in range(1, S):
        gains(d).wait_recv()
    gain = functools.reduce(lambda a, b: a + b, [n.gs[d] for d in range(S)])
    n.o_gqv[...] = gain[0:1]
    n.o_gkv[...] = gain[1:2]
    n.o_gqt[...] = gain[2:3]
    n.o_gkt[...] = gain[3:4]

    for d in range(1, G):
        tx(0, d).wait_send()
        tx(1, d).wait_send()
        tfin(d).wait_send()
        gainx(d).wait_send()
        for i in range(L):
            inp(i, d).wait_send()
            outp(0, i, d).wait_send()
            outp(1, i, d).wait_send()
    for p in range(2):
        for sem in (0, 1, 2, 5, 6, 7):
            tgat(p, sem, s, sib).wait_send()
        for half in range(2):
            trelay(p, half, s, sib).wait_send()
    for k in range(6):
        zred(k).wait_send()
    for z in range(Z):
        pair(z).wait_send()
    stat_pair().wait_send()
    for d in range(1, Z):
        stat(d).wait_send()
    for d in range(1, S):
        gains(d).wait_send()
    for i in range(LT):
        for up in (True, False):

            @pl.when((s < S - 1) if up else (s > 0))
            def _():
                halo(i, up).wait_send()
                hgrad(i, up).wait_send()


def hand_on(count, *refs):
    held = refs[2 * count : 3 * count]
    sem = refs[-1]
    copies = [
        (
            pltpu.make_async_copy(refs[k], held[k], sem.at[0, k]),
            pltpu.make_async_copy(held[k], refs[count + k], sem.at[1, k]),
        )
        for k in range(count)
    ]
    for one, _ in copies:
        one.start()
    for one, two in copies:
        one.wait()
        two.start()
    for _, two in copies:
        two.wait()


def body(S, G, *args):
    (q, k, v, g, qt, kt, vt, gt, gqv, gkv, gqt, gkt, windows, text_mask) = args
    R = q.shape[0]
    TD = qt.shape[0]
    TS = TD * G
    N = R * G
    L = HEADS // G
    LT = L // 2
    Z = S // 2
    smem = pl.BlockSpec(memory_space=pltpu.SMEM)
    vmem = pl.BlockSpec(memory_space=pltpu.VMEM)
    operands = [
        ("table", head_order(windows, G), smem),
        ("tmask", text_mask.reshape(1, TEXT), vmem),
        ("gqv", gqv.reshape(1, HD), vmem),
        ("gkv", gkv.reshape(1, HD), vmem),
        ("gqt", gqt.reshape(1, HD), vmem),
        ("gkt", gkt.reshape(1, HD), vmem),
        ("q", q, vmem),
        ("k", k, vmem),
        ("v", v, vmem),
        ("g", g, vmem),
        ("qt", qt, vmem),
        ("kt", kt, vmem),
        ("vt", vt, vmem),
        ("gt", gt, vmem),
    ]
    rows = jax.ShapeDtypeStruct((R, D), BF16)
    trows = jax.ShapeDtypeStruct((TD, D), BF16)
    gain = jax.ShapeDtypeStruct((1, HD), F32)
    outs = [
        ("o_out", rows),
        ("o_outt", trows),
        ("o_dq", rows),
        ("o_dk", rows),
        ("o_dv", rows),
        ("o_dqt", trows),
        ("o_dkt", trows),
        ("o_dvt", trows),
        ("o_gqv", gain),
        ("o_gkv", gain),
        ("o_gqt", gain),
        ("o_gkt", gain),
    ]
    V = pltpu.VMEM
    dma = pltpu.SemaphoreType.DMA
    K = 3 * N + TEXT
    scratch = [
        ("raw", V((HEADS, 4, R, HD), BF16)),
        ("rawt", V((4, HEADS, TD, HD), F32)),
        ("normt", V((2, HEADS, TD, HD), F32)),
        ("rawp", V((2, HEADS, TD, HD), F32)),
        ("tres", V((4, HEADS, TD, HD), F32)),
        ("swap", V((HD, HD), BF16)),
        ("mean", V((2 * HD, HD), BF16)),
        ("cos", V((R, HD), F32)),
        ("sin", V((R, HD), F32)),
        ("gcos", V((2, R, HD), F32)),
        ("gsin", V((2, R, HD), F32)),
        ("tbias", V((TEXT, HD), BF16)),
        ("tsend", V((2, G, L, 2 * TD, HD), BF16)),
        ("tg0", V((S, G, L, 2 * TD, HD), BF16)),
        ("tg1", V((S, G, L, 2 * TD, HD), BF16)),
        ("text", V((L, 4, TEXT, HD), BF16)),
        ("send", V((L, G, 4, R, HD), BF16)),
        ("recv", V((L, 4, N, HD), BF16)),
        ("halo", V((LT, 2, 2, N, HD), BF16)),
        ("hsend", V((LT, 2, 2, N, HD), BF16)),
        ("hrecv", V((LT, 2, 2, N, HD), BF16)),
        ("osend", V((2, L, G, 2, R, HD), BF16)),
        ("orecv0", V((HEADS, 2, R, HD), BF16)),
        ("orecv1", V((HEADS, 2, R, HD), BF16)),
        ("stats", V((2, 3, 8, TEXT), F32)),
        ("chips", V((Z, 3, 8, TEXT), F32)),
        ("tpart", V((S, 4, L, TS, HD), BF16)),
        ("tsib", V((Z, 4, L, TS, HD), BF16)),
        ("tz", V((Z, 4, L, TS, HD), BF16)),
        ("tzr", V((2, 4, L, TS, HD), BF16)),
        ("tzh", V((2, 2, L, TS, HD), BF16)),
        ("tfs", V((G, L, 2, 2 * TD, HD), BF16)),
        ("tfr", V((HEADS, 2, 2 * TD, HD), BF16)),
        ("gx", V((G, 8, HD), F32)),
        ("gs", V((S, 8, HD), F32)),
        ("qaug", V((N, 2 * HD), BF16)),
        ("kaug", V((K, 2 * HD), BF16)),
        ("vbuf", V((K, HD), BF16)),
        ("kT", V((HD, K), BF16)),
        ("vT", V((HD, K), BF16)),
        ("sbuf", V((K, 256), F32)),
        ("dvm", V((L, N, HD), F32)),
        ("dkm", V((L, N, HD), F32)),
        ("dvt", V((L, TEXT, HD), F32)),
        ("dkt", V((L, TEXT, HD), F32)),
        ("dvh", V((2 * N, HD), F32)),
        ("dkh", V((2 * N, HD), F32)),
        ("tx_s", dma((2, G))),
        ("tx_r", dma((2, G))),
        ("tg_s", dma((2, 8))),
        ("tg_r", dma((2, S + 2))),
        ("in_s", dma((L, G))),
        ("in_r", dma((L, G))),
        ("ha_s", dma((LT, 2))),
        ("ha_r", dma((LT, 2))),
        ("hg_s", dma((LT, 2))),
        ("hg_r", dma((LT, 2))),
        ("o_s", dma((2, L, G))),
        ("o_r", dma((2, L, G))),
        ("st_s", dma((Z,))),
        ("st_r", dma((Z,))),
        ("p_s", dma((Z,))),
        ("p_r", dma((Z,))),
        ("z_s", dma((6,))),
        ("z_r", dma((6,))),
        ("tf_s", dma((G,))),
        ("tf_r", dma((G,))),
        ("gx_s", dma((G,))),
        ("gx_r", dma((G,))),
        ("gs_s", dma((S,))),
        ("gs_r", dma((S,))),
    ]
    names = [o[0] for o in operands] + [o[0] for o in outs] + [o[0] for o in scratch]
    result = pl.pallas_call(
        functools.partial(kernel, S, G, names),
        out_shape=[o[1] for o in outs],
        in_specs=[o[2] for o in operands],
        out_specs=[vmem] * len(outs),
        scratch_shapes=[o[1] for o in scratch],
        compiler_params=pltpu.CompilerParams(
            collective_id=0, has_side_effects=True, vmem_limit_bytes=60 << 20
        ),
        cost_estimate=pl.CostEstimate(
            flops=7 * 10**9, bytes_accessed=7 * 10**6, transcendentals=5 * 10**6
        ),
    )(*[o[1] for o in operands])
    here = pl.BlockSpec(memory_space=pl.ANY)
    result = pl.pallas_call(
        functools.partial(hand_on, len(outs)),
        out_shape=[o[1] for o in outs],
        in_specs=[here] * len(outs),
        out_specs=[here] * len(outs),
        scratch_shapes=[V(o[1].shape, o[1].dtype) for o in outs] + [dma((2, len(outs)))],
    )(*result)
    return tuple(result[:8]) + tuple(r.reshape(HD) for r in result[8:])


def solution(mesh):
    S = mesh.shape["slab"]
    G = mesh.shape["heads"]
    rows = P(("replica", "slab", "heads"), None)
    split = P("replica")
    return jax.shard_map(
        functools.partial(body, S, G),
        mesh=mesh,
        in_specs=(rows,) * 8 + (split,) * 4 + (P(), split),
        out_specs=(rows,) * 8 + (split,) * 4,
        check_vma=False,
    )
```

```python
import functools

import jax
import jax.numpy as jnp
from jax import lax
from jax.experimental import pallas as pl
from jax.experimental.pallas import tpu as pltpu
from jax.sharding import PartitionSpec as P

HEADS = 24
HD = 128
D = 3072
TEXT = 256
GRID_H = 16
GRID_W = 32

EPSILON = 1e-06
ROPE_BASE = 256.0
NEGATIVE = -1e30
MANY = 6
FACTOR = HD ** (-0.5)
LOG2E = 1.4426950408889634
SHARP = FACTOR * LOG2E
MESH = pl.DeviceIdType.MESH
F32 = jnp.float32
BF16 = jnp.bfloat16


def head_order(windows, groups):
    local = HEADS // groups
    wide = windows[:, 0] == 3
    ids = jnp.arange(HEADS, dtype=jnp.int32)
    before = ids[None, :] < ids[:, None]
    rank_wide = jnp.sum(before & wide[None, :], axis=1, dtype=jnp.int32)
    rank_flat = jnp.sum(before & ~wide[None, :], axis=1, dtype=jnp.int32)
    slot = jnp.where(wide, rank_wide // groups, local // 2 + rank_flat // groups)
    group = jnp.where(wide, rank_wide % groups, rank_flat % groups)
    place = group * local + slot
    code = ids + windows[:, 1] // 2 * 32 + windows[:, 2] // 2 * 64
    chosen = place[None, :] == ids[:, None]
    code = jnp.sum(jnp.where(chosen, code[None, :], 0), axis=1, dtype=jnp.int32)
    return code + place * 128


def nt(a, b):
    return lax.dot_general(a, b, (((1,), (1,)), ((), ())), preferred_element_type=F32)


def nn(a, b):
    return lax.dot_general(a, b, (((1,), (0,)), ((), ())), preferred_element_type=F32)


def fold(values, op):
    return op(values.reshape(values.shape[0] // 8, 8, values.shape[1]), axis=0)


def partner_lane(lane):
    first = ((lane >= 16) & (lane < 44)) | ((lane >= 72) & (lane < 100))
    small = jnp.where(lane < 8, lane + 8, lane - 8)
    return jnp.where(lane < 16, small, jnp.where(first, lane + 28, lane - 28))


def partner(u):
    lane = lax.broadcasted_iota(jnp.int32, u.shape, 1)
    first = ((lane >= 16) & (lane < 44)) | ((lane >= 72) & (lane < 100))
    small = jnp.where(lane < 8, pltpu.roll(u, HD - 8, 1), pltpu.roll(u, 8, 1))
    large = jnp.where(first, pltpu.roll(u, HD - 28, 1), pltpu.roll(u, 28, 1))
    return jnp.where(lane < 16, small, large)


def rope_tables(frame, first_row, rows):
    lane = lax.broadcasted_iota(jnp.int32, (rows, HD), 1)
    row = lax.broadcasted_iota(jnp.int32, (rows, HD), 0)
    short = lane < 16
    middle = lane < 72
    inside = jnp.where(short, lane, jnp.where(middle, lane - 16, lane - 72))
    half = jnp.where(short, 8, 28)
    offset = jnp.where(inside >= half, inside - half, inside)
    place = jnp.where(short, frame, jnp.where(middle, first_row + row // GRID_W, lax.rem(row, GRID_W)))
    rate = jnp.where(short, -1.0, -16.0 / 56.0)
    angle = place.astype(F32) * jnp.exp2(offset.astype(F32) * rate)
    sine = jnp.sin(angle)
    return jnp.cos(angle), jnp.where(inside < half, -sine, sine)


class Names:
    pass


def kernel(S, G, names, *refs):
    n = Names()
    for name, ref in zip(names, refs):
        setattr(n, name, ref)
    n.orecv = (n.orecv0, n.orecv1)
    L = HEADS // G
    LT = L // 2
    R = n.q.shape[0]
    N = R * G
    TD = n.qt.shape[0]
    TS = TD * G
    Z = S // 2
    s = lax.axis_index("slab")
    x = lax.axis_index("heads")
    zi = s // 2
    ci = lax.rem(s, 2)
    sib = s + 1 - 2 * ci

    def xdev(d):
        return lax.rem(x + d, G)

    def sdev(d):
        return lax.rem(s + d, S)

    def zdev(d):
        return lax.rem(zi + d, Z) * 2 + ci

    def copy(src, dst, ss, rs, dev):
        return pltpu.make_async_remote_copy(
            src_ref=src, dst_ref=dst, send_sem=ss, recv_sem=rs, device_id=dev, device_id_type=MESH
        )

    bar = pltpu.get_barrier_semaphore()
    for d in range(1, G):
        pl.semaphore_signal(bar, inc=1, device_id={"heads": xdev(d)}, device_id_type=MESH)
    for d in range(1, S):
        pl.semaphore_signal(bar, inc=1, device_id={"slab": sdev(d)}, device_id_type=MESH)

    tg = (n.tg0, n.tg1)

    def tx(p, d):
        return copy(
            n.tsend.at[p, d], tg[p].at[s, x], n.tx_s.at[p, d], n.tx_r.at[p, d], {"heads": xdev(d)}
        )

    def tx_in(p, d):
        src = lax.rem(x + G - d, G)
        return copy(
            n.tsend.at[p, d], tg[p].at[s, src], n.tx_s.at[p, d], n.tx_r.at[p, d], {"heads": src}
        )

    def tgat(p, sem, slab, dev):
        return copy(
            tg[p].at[slab], tg[p].at[slab], n.tg_s.at[p, sem], n.tg_r.at[p, slab], {"slab": dev}
        )

    def trelay(p, half, src, dev):
        rows = tg[p].at[src, pl.ds(half * (G // 2), G // 2)]
        return copy(rows, rows, n.tg_s.at[p, 3 + half], n.tg_r.at[p, S + half], {"slab": dev})

    def inp(i, d):
        return copy(
            n.send.at[i, d],
            n.recv.at[i, :, pl.ds(pl.multiple_of(x * R, R), R), :],
            n.in_s.at[i, d],
            n.in_r.at[i, d],
            {"heads": xdev(d)},
        )

    def inp_in(i, d):
        src = lax.rem(x + G - d, G)
        return copy(
            n.send.at[i, d],
            n.recv.at[i, :, pl.ds(pl.multiple_of(src * R, R), R), :],
            n.in_s.at[i, d],
            n.in_r.at[i, d],
            {"heads": src},
        )

    def halo(i, up):
        return copy(
            n.recv.at[i, pl.ds(1, 2)],
            n.halo.at[i, 0 if up else 1],
            n.ha_s.at[i, 1 if up else 0],
            n.ha_r.at[i, 0 if up else 1],
            {"slab": s + 1 if up else s - 1},
        )

    def halo_in(i, below):
        k = 0 if below else 1
        return copy(
            n.recv.at[i, pl.ds(1, 2)],
            n.halo.at[i, k],
            n.ha_s.at[i, k],
            n.ha_r.at[i, k],
            {"slab": s - 1 if below else s + 1},
        )

    def hgrad(i, up):
        k = 1 if up else 0
        return copy(
            n.hsend.at[i, k],
            n.hrecv.at[i, 1 - k],
            n.hg_s.at[i, k],
            n.hg_r.at[i, 1 - k],
            {"slab": s + 1 if up else s - 1},
        )

    def hgrad_in(i, below):
        k = 0 if below else 1
        return copy(
            n.hsend.at[i, k],
            n.hrecv.at[i, k],
            n.hg_s.at[i, k],
            n.hg_r.at[i, k],
            {"slab": s - 1 if below else s + 1},
        )

    def outp(a, i, d):
        j = xdev(d)
        return copy(
            n.osend.at[a, i, j],
            n.orecv[a].at[x * L + i],
            n.o_s.at[a, i, d],
            n.o_r.at[a, i, d],
            {"heads": j},
        )

    def outp_in(a, i, d):
        src = lax.rem(x + G - d, G)
        return copy(
            n.osend.at[a, i, src],
            n.orecv[a].at[src * L + i],
            n.o_s.at[a, i, d],
            n.o_r.at[a, i, d],
            {"heads": src},
        )

    def stat_pair():
        return copy(n.stats.at[0], n.stats.at[1], n.st_s.at[0], n.st_r.at[0], {"slab": sib})

    def stat(d):
        at = n.chips.at[zi]
        return copy(at, at, n.st_s.at[d], n.st_r.at[d], {"slab": zdev(d)})

    def stat_in(d):
        src = lax.rem(zi + Z - d, Z)
        at = n.chips.at[src]
        return copy(at, at, n.st_s.at[d], n.st_r.at[d], {"slab": src * 2 + ci})

    def pair(z):
        return copy(
            n.tpart.at[2 * z + 1 - ci], n.tsib.at[z], n.p_s.at[z], n.p_r.at[z], {"slab": sib}
        )

    def zred(k):
        up = k % 2 == 0
        to = lax.rem(zi + (1 if up else Z - 1), Z)
        low = k in (0, 3, 4)
        rows = pl.ds(0 if low else 2, 2)
        if k < 2:
            src, dst = n.tz.at[lax.rem(zi + 2, Z), rows], n.tzh.at[k]
        else:
            src, dst = n.tz.at[to, rows], n.tzr.at[k % 2, rows]
        return copy(src, dst, n.z_s.at[k], n.z_r.at[k], {"slab": to * 2 + ci})

    def tfin(d):
        return copy(
            n.tfs.at[xdev(d)],
            n.tfr.at[pl.ds(x * L, L)],
            n.tf_s.at[d],
            n.tf_r.at[d],
            {"heads": xdev(d)},
        )

    def tfin_in(d):
        src = lax.rem(x + G - d, G)
        return copy(
            n.tfs.at[src], n.tfr.at[pl.ds(src * L, L)], n.tf_s.at[d], n.tf_r.at[d], {"heads": src}
        )

    def gainx(d):
        return copy(n.gx.at[0], n.gx.at[d], n.gx_s.at[d], n.gx_r.at[d], {"heads": xdev(d)})

    def gains(d):
        return copy(n.gs.at[0], n.gs.at[d], n.gs_s.at[d], n.gs_r.at[d], {"slab": sdev(d)})

    def order(p):
        return n.table[p] & 31

    def place(h):
        return n.table[h] >> 7

    def lanes(h):
        return pl.ds(pl.multiple_of(h * HD, HD), HD)

    def by_head(h, carry):
        for a, ref in enumerate((n.q, n.k, n.v, n.g)):
            n.raw[h, a] = ref[:, lanes(h)]
        return carry

    for h in range(HEADS):
        for a, ref in enumerate((n.qt, n.kt, n.vt, n.gt)):
            n.rawt[a, h] = ref[:, h * HD : (h + 1) * HD].astype(F32)

    k_lane = lax.broadcasted_iota(jnp.int32, (HD, HD), 0)
    lane = lax.broadcasted_iota(jnp.int32, (HD, HD), 1)
    n.swap[...] = jnp.where(k_lane == partner_lane(lane), 1.0, 0.0).astype(BF16)
    n.mean[...] = jnp.full((2 * HD, HD), 1.0 / HD, BF16)
    bias = jnp.where(n.tmask[...] == 1, 0.0, NEGATIVE)
    n.tbias[...] = jnp.broadcast_to(bias, (HD, TEXT)).T.astype(BF16)

    def lane_mean(values):
        high = values.astype(BF16)
        low = (values - high.astype(F32)).astype(BF16)
        return nn(jnp.concatenate([high, low], axis=1), n.mean[...])

    def inverse_rms(u):
        return lax.rsqrt(lane_mean(u * u) + EPSILON)

    for a, gain in ((0, n.gqt), (1, n.gkt)):
        u = n.rawt[a].reshape(HEADS * TD, HD)
        n.normt[a] = (u * inverse_rms(u) * gain[...]).reshape(HEADS, TD, HD)

    def text_pre(i, carry):
        for d in range(G):
            h = order(xdev(d) * L + i)
            rows = (
                jnp.concatenate([n.normt[1, h], n.rawt[2, h]], axis=0).astype(BF16),
                jnp.concatenate([n.normt[0, h], n.rawt[3, h]], axis=0).astype(BF16),
            )
            for p in range(2):
                if d == 0:
                    tg[p][s, x, i] = rows[p]
                else:
                    n.tsend[p, d, i] = rows[p]
        return carry

    lax.fori_loop(0, L, text_pre, 0)
    pl.semaphore_wait(bar, G - 1 + S - 1)
    for p in range(2):
        for d in range(1, G):
            tx(p, d).start()
    lax.fori_loop(0, HEADS, by_head, 0)
    cos, sin = rope_tables(s, x * (R // GRID_W), R)
    n.cos[...] = cos
    n.sin[...] = sin
    for k, gain in ((0, n.gqv), (1, n.gkv)):
        n.gcos[k] = gain[...] * cos
        n.gsin[k] = partner(jnp.broadcast_to(gain[...], (8, HD)))[0:1] * sin
    def normed(u, k):
        f = u.astype(F32)
        y = f * n.gcos[k] + nn(u, n.swap[...]) * n.gsin[k]
        return (y * inverse_rms(f)).astype(BF16)

    def video_pre(i, carry):
        for d in range(G):
            h = order(xdev(d) * L + i)
            rows = (normed(n.raw[h, 0], 0), normed(n.raw[h, 1], 1), n.raw[h, 2], n.raw[h, 3])
            for a in range(4):
                if d == 0:
                    n.recv[i, a, pl.ds(pl.multiple_of(x * R, R), R), :] = rows[a]
                else:
                    n.send[i, d, a] = rows[a]
        return carry

    def send_slot(i):
        for d in range(1, G):
            inp(i, d).start()

    after, behind, across = zdev(1), zdev(Z - 1), zdev(2)

    def text_out(p):
        for d in range(1, G):
            tx_in(p, d).wait_recv()
        tgat(p, 1, s, after).start()
        tgat(p, 2, s, behind).start()
        tgat(p, 0, s, sib).start()

    def text_relay(p):
        tgat(p, 1, behind, behind).wait_recv()
        trelay(p, 0, behind, after).start()
        tgat(p, 5, behind, sib).start()
        tgat(p, 2, after, after).wait_recv()
        trelay(p, 1, after, behind).start()
        tgat(p, 6, after, sib).start()

    def text_forward(p):
        trelay(p, 0, across, behind).wait_recv()
        trelay(p, 1, across, after).wait_recv()
        tgat(p, 7, across, sib).start()

    def text_in(p):
        tgat(p, 0, sib, sib).wait_recv()
        for d in range(1, Z):
            other = lax.rem(zi + d, Z) * 2 + 1 - ci
            tgat(p, 0, other, sib).wait_recv()

        def text_take(i, carry):
            both = tg[p][:, :, i].astype(F32).reshape(S * G, 2 * TD, HD)
            for k in range(2):
                n.text[i, 2 * p + k] = (
                    both[:, k * TD : (k + 1) * TD].reshape(TEXT, HD).astype(BF16)
                )
            return carry

        lax.fori_loop(0, L, text_take, 0)

    lax.fori_loop(0, 1, video_pre, 0)
    send_slot(0)
    lax.fori_loop(1, 2, video_pre, 0)
    text_out(0)
    send_slot(1)
    lax.fori_loop(2, L, video_pre, 0)

    row = lax.broadcasted_iota(jnp.int32, (N, HD), 0)
    lane = lax.broadcasted_iota(jnp.int32, (N, HD), 1)
    tile_row = row // (N // 2)
    tile_col = lax.rem(row, GRID_W) // 8
    n.qaug[:, HD:] = jnp.where(lane == tile_row * 4 + tile_col, 1.0, 0.0).astype(BF16)

    def forward_halo(i):
        for d in range(1, G):
            inp_in(i, d).wait_recv()
        if i < 2:
            send_slot(2 * i + 2)
            send_slot(2 * i + 3)

        @pl.when(s < S - 1)
        def _():
            halo(i, True).start()

        @pl.when(s > 0)
        def _():
            halo(i, False).start()

    def key_rows(at, count, k_rows, v_rows, feature):
        n.kaug[at : at + count, :HD] = k_rows
        n.kaug[at : at + count, HD:] = feature
        n.vbuf[at : at + count, :] = v_rows

    def attend(i, chunks):
        reach_y = (n.table[x * L + i] >> 5) & 1
        reach_x = (n.table[x * L + i] >> 6) & 1
        fits = (jnp.abs(tile_row - lane // 4) <= reach_y) & (
            jnp.abs(tile_col - lax.rem(lane, 4)) <= reach_x
        )
        feature = jnp.where(fits, 0.0, NEGATIVE).astype(BF16)
        n.qaug[:, :HD] = n.recv[i, 0]
        key_rows(0, N, n.recv[i, 1], n.recv[i, 2], feature)
        key_rows(N, TEXT, n.text[i, 0], n.text[i, 1], n.tbias[...])
        if chunks > 3:
            for k, below in ((0, True), (1, False)):
                at = N + TEXT + k * N
                here = (s > 0) if below else (s < S - 1)

                @pl.when(here)
                def _():
                    halo_in(i, below).wait_recv()
                    key_rows(at, N, n.halo[i, k, 0], n.halo[i, k, 1], feature)

                @pl.when(jnp.logical_not(here))
                def _():
                    zero = jnp.zeros((N, HD), BF16)
                    key_rows(at, N, zero, zero, jnp.full((N, HD), NEGATIVE, BF16))

        for c in range(chunks):
            at = slice(c * 256, (c + 1) * 256)
            n.kT[:, at] = n.kaug[at, :HD].T
            n.vT[:, at] = n.vbuf[at, :].T

        def block(b, carry):
            at_q = pl.ds(pl.multiple_of(b * 256, 256), 256)
            qa = n.qaug[at_q, :]
            qn = n.qaug[at_q, :HD]
            gb = n.recv[i, 3, at_q, :]
            top = jnp.full((8, 256), NEGATIVE, F32)
            for c in range(chunks):
                at = slice(c * 256, (c + 1) * 256)
                sc = nt(n.kaug[at, :], qa)
                n.sbuf[at, :] = sc
                top = jnp.maximum(top, fold(sc, jnp.max))
            top = jnp.max(top, axis=0, keepdims=True) * SHARP
            total = jnp.zeros((8, 256), F32)
            acc = jnp.zeros((HD, 256), F32)
            for c in range(chunks):
                at = slice(c * 256, (c + 1) * 256)
                e = jnp.exp2(n.sbuf[at, :] * SHARP - top)
                n.sbuf[at, :] = e
                total = total + fold(e, jnp.sum)
                w = e.astype(BF16)
                acc = acc + nn(n.vT[:, at], w)
                dv = nn(w, gb)
                if c * 256 < N:
                    n.dvm[i, at, :] += dv
                elif c * 256 < N + TEXT:
                    n.dvt[i, :, :] += dv
                else:
                    n.dvh[c * 256 - N - TEXT : (c + 1) * 256 - N - TEXT, :] += dv
            inv = 1.0 / jnp.sum(total, axis=0, keepdims=True)
            out = (acc * inv).astype(BF16)
            gT = gb.astype(F32).T
            dot = jnp.sum(fold(gT * out.astype(F32), jnp.sum), axis=0, keepdims=True)
            dq = jnp.zeros((HD, 256), F32)
            for c in range(chunks):
                at = slice(c * 256, (c + 1) * 256)
                dp = nt(n.vbuf[at, :], gb)
                ds = ((n.sbuf[at, :] * inv) * (dp - dot)).astype(BF16)
                dq = dq + nn(n.kT[:, at], ds)
                dk = nn(ds, qn)
                if c * 256 < N:
                    n.dkm[i, at, :] += dk
                elif c * 256 < N + TEXT:
                    n.dkt[i, :, :] += dk
                else:
                    n.dkh[c * 256 - N - TEXT : (c + 1) * 256 - N - TEXT, :] += dk
            out = out.astype(F32).T.astype(BF16)
            dq = (dq * FACTOR).T.astype(BF16)
            for j in range(256 // R):
                n.osend[0, i, b * (256 // R) + j, 0] = out[j * R : (j + 1) * R]
                n.osend[0, i, b * (256 // R) + j, 1] = dq[j * R : (j + 1) * R]
            return carry

        n.dvm[i] = jnp.zeros((N, HD), F32)
        n.dkm[i] = jnp.zeros((N, HD), F32)
        n.dvt[i] = jnp.zeros((TEXT, HD), F32)
        n.dkt[i] = jnp.zeros((TEXT, HD), F32)
        if chunks > 3:
            n.dvh[...] = jnp.zeros((2 * N, HD), F32)
            n.dkh[...] = jnp.zeros((2 * N, HD), F32)
        lax.fori_loop(0, N // 256, block, 0)

        for d in range(1, G):
            outp(0, i, d).start()
        n.orecv[0][x * L + i] = n.osend[0, i, x]
        if chunks > 3:
            for k in range(2):
                n.hsend[i, k, 0] = (n.dkh[k * N : (k + 1) * N, :] * FACTOR).astype(BF16)
                n.hsend[i, k, 1] = n.dvh[k * N : (k + 1) * N, :].astype(BF16)

            @pl.when(s < S - 1)
            def _():
                hgrad(i, True).start()

            @pl.when(s > 0)
            def _():
                hgrad(i, False).start()

    share = pl.ds(pl.multiple_of(s * TS, TS), TS)
    share_bias = n.tbias[share, :].astype(F32)
    share_bias = jnp.concatenate([share_bias, share_bias], axis=1)

    def text_scores(i):
        sv = nt(n.recv[i, 1], n.text[i, 2])
        st = nt(n.text[i, 0, share, :], n.text[i, 2]) + share_bias
        pv = nt(n.recv[i, 2], n.text[i, 3])
        pt = nt(n.text[i, 1, share, :], n.text[i, 3])
        return sv, st, pv, pt

    def text_first(i, carry):
        sv, st, pv, pt = text_scores(i)
        top = jnp.maximum(fold(sv, jnp.max), fold(st, jnp.max))
        top = jnp.max(top, axis=0, keepdims=True)
        ev = jnp.exp2((sv - top) * SHARP)
        et = jnp.exp2((st - top) * SHARP)
        total = fold(ev, jnp.sum) + fold(et, jnp.sum)
        dot = fold(ev * pv, jnp.sum) + fold(et * pt, jnp.sum)
        n.stats[0, 0, pl.ds(i, 1), :] = top
        n.stats[0, 1, pl.ds(i, 1), :] = jnp.sum(total, axis=0, keepdims=True)
        n.stats[0, 2, pl.ds(i, 1), :] = jnp.sum(dot, axis=0, keepdims=True)
        return carry

    def text_second(i, carry):
        sv, st, pv, pt = text_scores(i)
        tops = [n.chips[k, 0, pl.ds(i, 1), :] for k in range(Z)]
        top = functools.reduce(jnp.maximum, tops)
        total = jnp.zeros((1, TEXT), F32)
        dot = jnp.zeros((1, TEXT), F32)
        for k in range(Z):
            scale = jnp.exp2((tops[k] - top) * SHARP)
            total = total + n.chips[k, 1, pl.ds(i, 1), :] * scale
            dot = dot + n.chips[k, 2, pl.ds(i, 1), :] * scale
        inv = 1.0 / total
        dot = dot * inv
        ev = jnp.exp2((sv - top) * SHARP)
        et = jnp.exp2((st - top) * SHARP)
        wv = ev.astype(BF16)
        wt = et.astype(BF16)
        dsv = (ev * inv * (pv - dot)).astype(BF16)
        dst = (et * inv * (pt - dot)).astype(BF16)
        qt_ = n.text[i, 2]
        gt_ = n.text[i, 3]
        n.dvm[i] += nn(wv, gt_)
        n.dkm[i] += nn(dsv, qt_)
        n.dvt[i, share, :] += nn(wt, gt_)
        n.dkt[i, share, :] += nn(dst, qt_)
        kt_ = n.recv[i, 1].T
        vt_ = n.recv[i, 2].T
        ktt = n.text[i, 0, share, :].astype(F32).T.astype(BF16)
        vtt = n.text[i, 1, share, :].astype(F32).T.astype(BF16)
        out = (nn(vt_, wv) + nn(vtt, wt)) * inv
        dq = (nn(kt_, dsv) + nn(ktt, dst)) * FACTOR
        n.tpart[:, 0, i] = out.T.astype(BF16).reshape(S, TS, HD)
        n.tpart[:, 1, i] = dq.T.astype(BF16).reshape(S, TS, HD)
        n.tpart[:, 2, i] = (n.dkt[i] * FACTOR).astype(BF16).reshape(S, TS, HD)
        n.tpart[:, 3, i] = n.dvt[i].astype(BF16).reshape(S, TS, HD)
        return carry

    forward_halo(0)
    text_relay(0)
    text_out(1)
    forward_halo(1)
    text_forward(0)
    text_in(0)

    def attend_pair(i, carry):
        attend(i, (3 * N + TEXT) // 256)

        @pl.when(i == 0)
        def _():
            forward_halo(2)
            text_relay(1)

        @pl.when(i == 1)
        def _():
            text_forward(1)

        for d in range(1, G):
            inp_in(LT + i, d).wait_recv()

        @pl.when(i == LT - 1)
        def _():
            text_in(1)
            n.stats[0] = jnp.zeros((3, 8, TEXT), F32)
            lax.fori_loop(0, L, text_first, 0)
            stat_pair().start()
            stat_pair().wait_recv()
            top = jnp.maximum(n.stats[0, 0], n.stats[1, 0])
            scales = [jnp.exp2((n.stats[k, 0] - top) * SHARP) for k in range(2)]
            n.chips[zi, 0] = top
            for a in (1, 2):
                n.chips[zi, a] = n.stats[0, a] * scales[0] + n.stats[1, a] * scales[1]
            for d in range(1, Z):
                stat(d).start()

        attend(LT + i, (N + TEXT) // 256)
        return carry

    lax.fori_loop(0, LT, attend_pair, 0)
    for d in range(1, Z):
        stat_in(d).wait_recv()

    def finish(i, wide):
        def pack(dk, dv):
            for j in range(G):
                n.osend[1, i, j, 0] = dk[j * R : (j + 1) * R].astype(BF16)
                n.osend[1, i, j, 1] = dv[j * R : (j + 1) * R].astype(BF16)

        if wide:
            for k, below in ((0, True), (1, False)):

                @pl.when((s > 0) if below else (s < S - 1))
                def _():
                    hgrad_in(i, below).wait_recv()
                    n.dkm[i] += n.hrecv[i, k, 0].astype(F32) * (1.0 / FACTOR)
                    n.dvm[i] += n.hrecv[i, k, 1].astype(F32)

        pack(n.dkm[i] * FACTOR, n.dvm[i])
        for d in range(1, G):
            outp(1, i, d).start()
        n.orecv[1][x * L + i] = n.osend[1, i, x]

    def finish_flat(i, carry):
        text_second(i, 0)
        finish(i, False)
        return carry

    def finish_wide(i, carry):
        finish(i, True)
        return carry

    def relay_sums():
        for k in range(2):
            to = lax.rem(zi + (1 if k == 0 else Z - 1), Z)
            rows = slice(2 * k, 2 * k + 2)
            zred(k).wait_recv()
            n.tz[to, rows] = (n.tz[to, rows].astype(F32) + n.tzh[k].astype(F32)).astype(BF16)
            zred(4 + k).start()

    lax.fori_loop(LT, L, finish_flat, 0)
    lax.fori_loop(0, LT, text_second, 0)
    for z in range(Z):
        pair(z).start()
    for z in range(Z):
        pair(z).wait_recv()
        n.tz[z] = (n.tpart[2 * z + ci].astype(F32) + n.tsib[z].astype(F32)).astype(BF16)
    for k in range(4):
        zred(k).start()
    lax.fori_loop(0, LT - 1, finish_wide, 0)
    relay_sums()
    lax.fori_loop(LT - 1, LT, finish_wide, 0)

    for i in range(L):
        for d in range(1, G):
            outp_in(0, i, d).wait_recv()

    def norm_back(u, dy, gain):
        f = u.astype(F32)
        r = inverse_rms(f)
        unit = f * r
        part = dy * unit
        return r * (dy * gain - unit * lane_mean(part * gain)), part

    cos_many = jnp.concatenate([n.cos[...]] * MANY, axis=0)
    sin_many = jnp.concatenate([n.sin[...]] * MANY, axis=0)

    def post(step, carry, received, back, plain, source, gain, out_plain, out_grad):
        heads = [MANY * step + k for k in range(MANY)]
        places = [place(h) for h in heads]
        for h, p in zip(heads, places):
            out_plain[:, lanes(h)] = received[p, plain]
        y = jnp.concatenate([received[p, back] for p in places], axis=0)
        u = jnp.concatenate([source[:, lanes(h)] for h in heads], axis=0)
        dy = y.astype(F32) * cos_many - nn(y, n.swap[...]) * sin_many
        grad, part = norm_back(u, dy, gain[...])
        for k, h in enumerate(heads):
            out_grad[:, lanes(h)] = grad[k * R : (k + 1) * R].astype(BF16)
        return carry + fold(part, jnp.sum)

    def post_q(step, carry):
        return post(step, carry, n.orecv[0], 1, 0, n.q, n.gqv, n.o_out, n.o_dq)

    def post_k(step, carry):
        return post(step, carry, n.orecv[1], 0, 1, n.k, n.gkv, n.o_dv, n.o_dk)

    zero = jnp.zeros((8, HD), F32)
    gain_qv = lax.fori_loop(0, HEADS // MANY, post_q, zero)

    for k in range(2, 6):
        zred(k).wait_recv()
    summed = n.tz[zi].astype(F32) + n.tzr[0].astype(F32) + n.tzr[1].astype(F32)
    for j in range(G):
        rows = slice(j * TD, (j + 1) * TD)
        for p in range(2):
            n.tfs[j, :, p] = jnp.concatenate(
                [summed[2 * p, :, rows], summed[2 * p + 1, :, rows]], axis=1
            ).astype(BF16)
    for d in range(1, G):
        tfin(d).start()
    n.tfr[pl.ds(x * L, L)] = n.tfs[x]

    for i in range(L):
        for d in range(1, G):
            outp_in(1, i, d).wait_recv()

    gain_kv = lax.fori_loop(0, HEADS // MANY, post_k, zero)

    def text_order(p, carry):
        h = order(p)
        n.rawp[0, p] = n.rawt[0, h]
        n.rawp[1, p] = n.rawt[1, h]
        return carry

    lax.fori_loop(0, HEADS, text_order, 0)
    for d in range(1, G):
        tfin_in(d).wait_recv()

    first = n.tfr[:, 0].astype(F32)
    second = n.tfr[:, 1].astype(F32)
    n.tres[0] = first[:, :TD]
    n.tres[3] = second[:, TD:]
    gain_t = []
    for k, dy, gain in ((0, first[:, TD:], n.gqt), (1, second[:, :TD], n.gkt)):
        u = n.rawp[k].reshape(HEADS * TD, HD)
        grad, part = norm_back(u, dy.reshape(HEADS * TD, HD), gain[...])
        n.tres[1 + k] = grad.reshape(HEADS, TD, HD)
        gain_t.append(fold(part, jnp.sum))

    def post_t(h, carry):
        p = place(h)
        n.o_outt[:, lanes(h)] = n.tres[0, p].astype(BF16)
        n.o_dqt[:, lanes(h)] = n.tres[1, p].astype(BF16)
        n.o_dkt[:, lanes(h)] = n.tres[2, p].astype(BF16)
        n.o_dvt[:, lanes(h)] = n.tres[3, p].astype(BF16)
        return carry

    parts = [
        jnp.sum(part, axis=0, keepdims=True) for part in (gain_qv, gain_kv, *gain_t)
    ]
    n.gx[0] = jnp.concatenate(parts + [jnp.zeros((4, HD), F32)], axis=0)
    for d in range(1, G):
        gainx(d).start()
    lax.fori_loop(0, HEADS, post_t, 0)
    for d in range(1, G):
        gainx(d).wait_recv()
    n.gs[0] = functools.reduce(lambda a, b: a + b, [n.gx[d] for d in range(G)])
    for d in range(1, S):
        gains(d).start()
    for d in range(1, S):
        gains(d).wait_recv()
    gain = functools.reduce(lambda a, b: a + b, [n.gs[d] for d in range(S)])
    n.o_gqv[...] = gain[0:1]
    n.o_gkv[...] = gain[1:2]
    n.o_gqt[...] = gain[2:3]
    n.o_gkt[...] = gain[3:4]

    for d in range(1, G):
        tx(0, d).wait_send()
        tx(1, d).wait_send()
        tfin(d).wait_send()
        gainx(d).wait_send()
        for i in range(L):
            inp(i, d).wait_send()
            outp(0, i, d).wait_send()
            outp(1, i, d).wait_send()
    for p in range(2):
        for sem in (0, 1, 2, 5, 6, 7):
            tgat(p, sem, s, sib).wait_send()
        for half in range(2):
            trelay(p, half, s, sib).wait_send()
    for k in range(6):
        zred(k).wait_send()
    for z in range(Z):
        pair(z).wait_send()
    stat_pair().wait_send()
    for d in range(1, Z):
        stat(d).wait_send()
    for d in range(1, S):
        gains(d).wait_send()
    for i in range(LT):
        for up in (True, False):

            @pl.when((s < S - 1) if up else (s > 0))
            def _():
                halo(i, up).wait_send()
                hgrad(i, up).wait_send()


def hand_on(count, *refs):
    held = refs[2 * count : 3 * count]
    sem = refs[-1]
    copies = [
        (
            pltpu.make_async_copy(refs[k], held[k], sem.at[0, k]),
            pltpu.make_async_copy(held[k], refs[count + k], sem.at[1, k]),
        )
        for k in range(count)
    ]
    for one, _ in copies:
        one.start()
    for one, two in copies:
        one.wait()
        two.start()
    for _, two in copies:
        two.wait()


def body(S, G, *args):
    (q, k, v, g, qt, kt, vt, gt, gqv, gkv, gqt, gkt, windows, text_mask) = args
    R = q.shape[0]
    TD = qt.shape[0]
    TS = TD * G
    N = R * G
    L = HEADS // G
    LT = L // 2
    Z = S // 2
    smem = pl.BlockSpec(memory_space=pltpu.SMEM)
    vmem = pl.BlockSpec(memory_space=pltpu.VMEM)
    operands = [
        ("table", head_order(windows, G), smem),
        ("tmask", text_mask.reshape(1, TEXT), vmem),
        ("gqv", gqv.reshape(1, HD), vmem),
        ("gkv", gkv.reshape(1, HD), vmem),
        ("gqt", gqt.reshape(1, HD), vmem),
        ("gkt", gkt.reshape(1, HD), vmem),
        ("q", q, vmem),
        ("k", k, vmem),
        ("v", v, vmem),
        ("g", g, vmem),
        ("qt", qt, vmem),
        ("kt", kt, vmem),
        ("vt", vt, vmem),
        ("gt", gt, vmem),
    ]
    rows = jax.ShapeDtypeStruct((R, D), BF16)
    trows = jax.ShapeDtypeStruct((TD, D), BF16)
    gain = jax.ShapeDtypeStruct((1, HD), F32)
    outs = [
        ("o_out", rows),
        ("o_outt", trows),
        ("o_dq", rows),
        ("o_dk", rows),
        ("o_dv", rows),
        ("o_dqt", trows),
        ("o_dkt", trows),
        ("o_dvt", trows),
        ("o_gqv", gain),
        ("o_gkv", gain),
        ("o_gqt", gain),
        ("o_gkt", gain),
    ]
    V = pltpu.VMEM
    dma = pltpu.SemaphoreType.DMA
    K = 3 * N + TEXT
    scratch = [
        ("raw", V((HEADS, 4, R, HD), BF16)),
        ("rawt", V((4, HEADS, TD, HD), F32)),
        ("normt", V((2, HEADS, TD, HD), F32)),
        ("rawp", V((2, HEADS, TD, HD), F32)),
        ("tres", V((4, HEADS, TD, HD), F32)),
        ("swap", V((HD, HD), BF16)),
        ("mean", V((2 * HD, HD), BF16)),
        ("cos", V((R, HD), F32)),
        ("sin", V((R, HD), F32)),
        ("gcos", V((2, R, HD), F32)),
        ("gsin", V((2, R, HD), F32)),
        ("tbias", V((TEXT, HD), BF16)),
        ("tsend", V((2, G, L, 2 * TD, HD), BF16)),
        ("tg0", V((S, G, L, 2 * TD, HD), BF16)),
        ("tg1", V((S, G, L, 2 * TD, HD), BF16)),
        ("text", V((L, 4, TEXT, HD), BF16)),
        ("send", V((L, G, 4, R, HD), BF16)),
        ("recv", V((L, 4, N, HD), BF16)),
        ("halo", V((LT, 2, 2, N, HD), BF16)),
        ("hsend", V((LT, 2, 2, N, HD), BF16)),
        ("hrecv", V((LT, 2, 2, N, HD), BF16)),
        ("osend", V((2, L, G, 2, R, HD), BF16)),
        ("orecv0", V((HEADS, 2, R, HD), BF16)),
        ("orecv1", V((HEADS, 2, R, HD), BF16)),
        ("stats", V((2, 3, 8, TEXT), F32)),
        ("chips", V((Z, 3, 8, TEXT), F32)),
        ("tpart", V((S, 4, L, TS, HD), BF16)),
        ("tsib", V((Z, 4, L, TS, HD), BF16)),
        ("tz", V((Z, 4, L, TS, HD), BF16)),
        ("tzr", V((2, 4, L, TS, HD), BF16)),
        ("tzh", V((2, 2, L, TS, HD), BF16)),
        ("tfs", V((G, L, 2, 2 * TD, HD), BF16)),
        ("tfr", V((HEADS, 2, 2 * TD, HD), BF16)),
        ("gx", V((G, 8, HD), F32)),
        ("gs", V((S, 8, HD), F32)),
        ("qaug", V((N, 2 * HD), BF16)),
        ("kaug", V((K, 2 * HD), BF16)),
        ("vbuf", V((K, HD), BF16)),
        ("kT", V((HD, K), BF16)),
        ("vT", V((HD, K), BF16)),
        ("sbuf", V((K, 256), F32)),
        ("dvm", V((L, N, HD), F32)),
        ("dkm", V((L, N, HD), F32)),
        ("dvt", V((L, TEXT, HD), F32)),
        ("dkt", V((L, TEXT, HD), F32)),
        ("dvh", V((2 * N, HD), F32)),
        ("dkh", V((2 * N, HD), F32)),
        ("tx_s", dma((2, G))),
        ("tx_r", dma((2, G))),
        ("tg_s", dma((2, 8))),
        ("tg_r", dma((2, S + 2))),
        ("in_s", dma((L, G))),
        ("in_r", dma((L, G))),
        ("ha_s", dma((LT, 2))),
        ("ha_r", dma((LT, 2))),
        ("hg_s", dma((LT, 2))),
        ("hg_r", dma((LT, 2))),
        ("o_s", dma((2, L, G))),
        ("o_r", dma((2, L, G))),
        ("st_s", dma((Z,))),
        ("st_r", dma((Z,))),
        ("p_s", dma((Z,))),
        ("p_r", dma((Z,))),
        ("z_s", dma((6,))),
        ("z_r", dma((6,))),
        ("tf_s", dma((G,))),
        ("tf_r", dma((G,))),
        ("gx_s", dma((G,))),
        ("gx_r", dma((G,))),
        ("gs_s", dma((S,))),
        ("gs_r", dma((S,))),
    ]
    names = [o[0] for o in operands] + [o[0] for o in outs] + [o[0] for o in scratch]
    result = pl.pallas_call(
        functools.partial(kernel, S, G, names),
        out_shape=[o[1] for o in outs],
        in_specs=[o[2] for o in operands],
        out_specs=[vmem] * len(outs),
        scratch_shapes=[o[1] for o in scratch],
        compiler_params=pltpu.CompilerParams(
            collective_id=0, has_side_effects=True, vmem_limit_bytes=60 << 20
        ),
        cost_estimate=pl.CostEstimate(
            flops=7 * 10**9, bytes_accessed=7 * 10**6, transcendentals=5 * 10**6
        ),
    )(*[o[1] for o in operands])
    here = pl.BlockSpec(memory_space=pl.ANY)
    result = pl.pallas_call(
        functools.partial(hand_on, len(outs)),
        out_shape=[o[1] for o in outs],
        in_specs=[here] * len(outs),
        out_specs=[here] * len(outs),
        scratch_shapes=[V(o[1].shape, o[1].dtype) for o in outs] + [dma((2, len(outs)))],
    )(*result)
    return tuple(result[:8]) + tuple(r.reshape(HD) for r in result[8:])


def solution(mesh):
    S = mesh.shape["slab"]
    G = mesh.shape["heads"]
    rows = P(("replica", "slab", "heads"), None)
    split = P("replica")
    return jax.shard_map(
        functools.partial(body, S, G),
        mesh=mesh,
        in_specs=(rows,) * 8 + (split,) * 4 + (P(), split),
        out_specs=(rows,) * 8 + (split,) * 4,
        check_vma=False,
    )
```

```python
import functools

import jax
import jax.numpy as jnp
from jax import lax
from jax.experimental import pallas as pl
from jax.experimental.pallas import tpu as pltpu
from jax.sharding import PartitionSpec as P

HEADS = 24
HD = 128
D = 3072
TEXT = 256
GRID_H = 16
GRID_W = 32

EPSILON = 1e-06
ROPE_BASE = 256.0
NEGATIVE = -1e30
MANY = 6
FACTOR = HD ** (-0.5)
LOG2E = 1.4426950408889634
SHARP = FACTOR * LOG2E
MESH = pl.DeviceIdType.MESH
F32 = jnp.float32
BF16 = jnp.bfloat16


def head_order(windows, groups):
    local = HEADS // groups
    wide = windows[:, 0] == 3
    ids = jnp.arange(HEADS, dtype=jnp.int32)
    before = ids[None, :] < ids[:, None]
    rank_wide = jnp.sum(before & wide[None, :], axis=1, dtype=jnp.int32)
    rank_flat = jnp.sum(before & ~wide[None, :], axis=1, dtype=jnp.int32)
    slot = jnp.where(wide, rank_wide // groups, local // 2 + rank_flat // groups)
    group = jnp.where(wide, rank_wide % groups, rank_flat % groups)
    place = group * local + slot
    code = ids + windows[:, 1] // 2 * 32 + windows[:, 2] // 2 * 64
    chosen = place[None, :] == ids[:, None]
    code = jnp.sum(jnp.where(chosen, code[None, :], 0), axis=1, dtype=jnp.int32)
    return code + place * 128


def nt(a, b):
    return lax.dot_general(a, b, (((1,), (1,)), ((), ())), preferred_element_type=F32)


def nn(a, b):
    return lax.dot_general(a, b, (((1,), (0,)), ((), ())), preferred_element_type=F32)


def fold(values, op):
    return op(values.reshape(values.shape[0] // 8, 8, values.shape[1]), axis=0)


def partner_lane(lane):
    first = ((lane >= 16) & (lane < 44)) | ((lane >= 72) & (lane < 100))
    small = jnp.where(lane < 8, lane + 8, lane - 8)
    return jnp.where(lane < 16, small, jnp.where(first, lane + 28, lane - 28))


def partner(u):
    lane = lax.broadcasted_iota(jnp.int32, u.shape, 1)
    first = ((lane >= 16) & (lane < 44)) | ((lane >= 72) & (lane < 100))
    small = jnp.where(lane < 8, pltpu.roll(u, HD - 8, 1), pltpu.roll(u, 8, 1))
    large = jnp.where(first, pltpu.roll(u, HD - 28, 1), pltpu.roll(u, 28, 1))
    return jnp.where(lane < 16, small, large)


def rope_tables(frame, first_row, rows):
    lane = lax.broadcasted_iota(jnp.int32, (rows, HD), 1)
    row = lax.broadcasted_iota(jnp.int32, (rows, HD), 0)
    short = lane < 16
    middle = lane < 72
    inside = jnp.where(short, lane, jnp.where(middle, lane - 16, lane - 72))
    half = jnp.where(short, 8, 28)
    offset = jnp.where(inside >= half, inside - half, inside)
    place = jnp.where(short, frame, jnp.where(middle, first_row + row // GRID_W, lax.rem(row, GRID_W)))
    rate = jnp.where(short, -1.0, -16.0 / 56.0)
    angle = place.astype(F32) * jnp.exp2(offset.astype(F32) * rate)
    sine = jnp.sin(angle)
    return jnp.cos(angle), jnp.where(inside < half, -sine, sine)


class Names:
    pass


def kernel(S, G, names, *refs):
    n = Names()
    for name, ref in zip(names, refs):
        setattr(n, name, ref)
    n.orecv = (n.orecv0, n.orecv1)
    L = HEADS // G
    LT = L // 2
    R = n.q.shape[0]
    N = R * G
    TD = n.qt.shape[0]
    TS = TD * G
    Z = S // 2
    s = lax.axis_index("slab")
    x = lax.axis_index("heads")
    zi = s // 2
    ci = lax.rem(s, 2)
    sib = s + 1 - 2 * ci

    def xdev(d):
        return lax.rem(x + d, G)

    def sdev(d):
        return lax.rem(s + d, S)

    def zdev(d):
        return lax.rem(zi + d, Z) * 2 + ci

    def copy(src, dst, ss, rs, dev):
        return pltpu.make_async_remote_copy(
            src_ref=src, dst_ref=dst, send_sem=ss, recv_sem=rs, device_id=dev, device_id_type=MESH
        )

    bar = pltpu.get_barrier_semaphore()
    for d in range(1, G):
        pl.semaphore_signal(bar, inc=1, device_id={"heads": xdev(d)}, device_id_type=MESH)
    for d in range(1, S):
        pl.semaphore_signal(bar, inc=1, device_id={"slab": sdev(d)}, device_id_type=MESH)

    tg = (n.tg0, n.tg1)

    def tx(p, d):
        return copy(
            n.tsend.at[p, d], tg[p].at[s, x], n.tx_s.at[p, d], n.tx_r.at[p, d], {"heads": xdev(d)}
        )

    def tx_in(p, d):
        src = lax.rem(x + G - d, G)
        return copy(
            n.tsend.at[p, d], tg[p].at[s, src], n.tx_s.at[p, d], n.tx_r.at[p, d], {"heads": src}
        )

    def tgat(p, sem, slab, dev):
        return copy(
            tg[p].at[slab], tg[p].at[slab], n.tg_s.at[p, sem], n.tg_r.at[p, slab], {"slab": dev}
        )

    def trelay(p, half, src, dev):
        rows = tg[p].at[src, pl.ds(half * (G // 2), G // 2)]
        return copy(rows, rows, n.tg_s.at[p, 3 + half], n.tg_r.at[p, S + half], {"slab": dev})

    def inp(i, d):
        return copy(
            n.send.at[i, d],
            n.recv.at[i, :, pl.ds(pl.multiple_of(x * R, R), R), :],
            n.in_s.at[i, d],
            n.in_r.at[i, d],
            {"heads": xdev(d)},
        )

    def inp_in(i, d):
        src = lax.rem(x + G - d, G)
        return copy(
            n.send.at[i, d],
            n.recv.at[i, :, pl.ds(pl.multiple_of(src * R, R), R), :],
            n.in_s.at[i, d],
            n.in_r.at[i, d],
            {"heads": src},
        )

    def halo(i, up):
        return copy(
            n.recv.at[i, pl.ds(1, 2)],
            n.halo.at[i, 0 if up else 1],
            n.ha_s.at[i, 1 if up else 0],
            n.ha_r.at[i, 0 if up else 1],
            {"slab": s + 1 if up else s - 1},
        )

    def halo_in(i, below):
        k = 0 if below else 1
        return copy(
            n.recv.at[i, pl.ds(1, 2)],
            n.halo.at[i, k],
            n.ha_s.at[i, k],
            n.ha_r.at[i, k],
            {"slab": s - 1 if below else s + 1},
        )

    def hgrad(i, up):
        k = 1 if up else 0
        return copy(
            n.hsend.at[i, k],
            n.hrecv.at[i, 1 - k],
            n.hg_s.at[i, k],
            n.hg_r.at[i, 1 - k],
            {"slab": s + 1 if up else s - 1},
        )

    def hgrad_in(i, below):
        k = 0 if below else 1
        return copy(
            n.hsend.at[i, k],
            n.hrecv.at[i, k],
            n.hg_s.at[i, k],
            n.hg_r.at[i, k],
            {"slab": s - 1 if below else s + 1},
        )

    def outp(a, i, d):
        j = xdev(d)
        return copy(
            n.osend.at[a, i, j],
            n.orecv[a].at[x * L + i],
            n.o_s.at[a, i, d],
            n.o_r.at[a, i, d],
            {"heads": j},
        )

    def outp_in(a, i, d):
        src = lax.rem(x + G - d, G)
        return copy(
            n.osend.at[a, i, src],
            n.orecv[a].at[src * L + i],
            n.o_s.at[a, i, d],
            n.o_r.at[a, i, d],
            {"heads": src},
        )

    def stat_pair():
        return copy(n.stats.at[0], n.stats.at[1], n.st_s.at[0], n.st_r.at[0], {"slab": sib})

    def stat(d):
        at = n.chips.at[zi]
        return copy(at, at, n.st_s.at[d], n.st_r.at[d], {"slab": zdev(d)})

    def stat_in(d):
        src = lax.rem(zi + Z - d, Z)
        at = n.chips.at[src]
        return copy(at, at, n.st_s.at[d], n.st_r.at[d], {"slab": src * 2 + ci})

    def pair(z):
        return copy(
            n.tpart.at[2 * z + 1 - ci], n.tsib.at[z], n.p_s.at[z], n.p_r.at[z], {"slab": sib}
        )

    def zred(k):
        up = k % 2 == 0
        to = lax.rem(zi + (1 if up else Z - 1), Z)
        low = k in (0, 3, 4)
        rows = pl.ds(0 if low else 2, 2)
        if k < 2:
            src, dst = n.tz.at[lax.rem(zi + 2, Z), rows], n.tzh.at[k]
        else:
            src, dst = n.tz.at[to, rows], n.tzr.at[k % 2, rows]
        return copy(src, dst, n.z_s.at[k], n.z_r.at[k], {"slab": to * 2 + ci})

    def tfin(d):
        return copy(
            n.tfs.at[xdev(d)],
            n.tfr.at[pl.ds(x * L, L)],
            n.tf_s.at[d],
            n.tf_r.at[d],
            {"heads": xdev(d)},
        )

    def tfin_in(d):
        src = lax.rem(x + G - d, G)
        return copy(
            n.tfs.at[src], n.tfr.at[pl.ds(src * L, L)], n.tf_s.at[d], n.tf_r.at[d], {"heads": src}
        )

    def gainx(d):
        return copy(n.gx.at[0], n.gx.at[d], n.gx_s.at[d], n.gx_r.at[d], {"heads": xdev(d)})

    def gains(d):
        return copy(n.gs.at[0], n.gs.at[d], n.gs_s.at[d], n.gs_r.at[d], {"slab": sdev(d)})

    def order(p):
        return n.table[p] & 31

    def place(h):
        return n.table[h] >> 7

    def lanes(h):
        return pl.ds(pl.multiple_of(h * HD, HD), HD)

    def by_head(h, carry):
        for a, ref in enumerate((n.q, n.k, n.v, n.g)):
            n.raw[h, a] = ref[:, lanes(h)]
        return carry

    for h in range(HEADS):
        for a, ref in enumerate((n.qt, n.kt, n.vt, n.gt)):
            n.rawt[a, h] = ref[:, h * HD : (h + 1) * HD].astype(F32)

    k_lane = lax.broadcasted_iota(jnp.int32, (HD, HD), 0)
    lane = lax.broadcasted_iota(jnp.int32, (HD, HD), 1)
    n.swap[...] = jnp.where(k_lane == partner_lane(lane), 1.0, 0.0).astype(BF16)
    n.mean[...] = jnp.full((2 * HD, HD), 1.0 / HD, BF16)
    bias = jnp.where(n.tmask[...] == 1, 0.0, NEGATIVE)
    n.tbias[...] = jnp.broadcast_to(bias, (HD, TEXT)).T.astype(BF16)

    def lane_mean(values):
        high = values.astype(BF16)
        low = (values - high.astype(F32)).astype(BF16)
        return nn(jnp.concatenate([high, low], axis=1), n.mean[...])

    def inverse_rms(u):
        return lax.rsqrt(lane_mean(u * u) + EPSILON)

    for a, gain in ((0, n.gqt), (1, n.gkt)):
        u = n.rawt[a].reshape(HEADS * TD, HD)
        n.normt[a] = (u * inverse_rms(u) * gain[...]).reshape(HEADS, TD, HD)

    def text_pre(i, carry):
        for d in range(G):
            h = order(xdev(d) * L + i)
            rows = (
                jnp.concatenate([n.normt[1, h], n.rawt[2, h]], axis=0).astype(BF16),
                jnp.concatenate([n.normt[0, h], n.rawt[3, h]], axis=0).astype(BF16),
            )
            for p in range(2):
                if d == 0:
                    tg[p][s, x, i] = rows[p]
                else:
                    n.tsend[p, d, i] = rows[p]
        return carry

    lax.fori_loop(0, L, text_pre, 0)
    pl.semaphore_wait(bar, G - 1 + S - 1)
    for p in range(2):
        for d in range(1, G):
            tx(p, d).start()
    lax.fori_loop(0, HEADS, by_head, 0)
    cos, sin = rope_tables(s, x * (R // GRID_W), R)
    n.cos[...] = cos
    n.sin[...] = sin
    for k, gain in ((0, n.gqv), (1, n.gkv)):
        n.gcos[k] = gain[...] * cos
        n.gsin[k] = partner(jnp.broadcast_to(gain[...], (8, HD)))[0:1] * sin
    def normed(u, k):
        f = u.astype(F32)
        y = f * n.gcos[k] + nn(u, n.swap[...]) * n.gsin[k]
        return (y * inverse_rms(f)).astype(BF16)

    def video_pre(i, carry):
        for d in range(G):
            h = order(xdev(d) * L + i)
            rows = (normed(n.raw[h, 0], 0), normed(n.raw[h, 1], 1), n.raw[h, 2], n.raw[h, 3])
            for a in range(4):
                if d == 0:
                    n.recv[i, a, pl.ds(pl.multiple_of(x * R, R), R), :] = rows[a]
                else:
                    n.send[i, d, a] = rows[a]
        return carry

    def send_slot(i):
        for d in range(1, G):
            inp(i, d).start()

    after, behind, across = zdev(1), zdev(Z - 1), zdev(2)

    def text_out(p):
        for d in range(1, G):
            tx_in(p, d).wait_recv()
        tgat(p, 1, s, after).start()
        tgat(p, 2, s, behind).start()
        tgat(p, 0, s, sib).start()

    def text_relay(p):
        tgat(p, 1, behind, behind).wait_recv()
        trelay(p, 0, behind, after).start()
        tgat(p, 5, behind, sib).start()
        tgat(p, 2, after, after).wait_recv()
        trelay(p, 1, after, behind).start()
        tgat(p, 6, after, sib).start()

    def text_forward(p):
        trelay(p, 0, across, behind).wait_recv()
        trelay(p, 1, across, after).wait_recv()
        tgat(p, 7, across, sib).start()

    def text_in(p):
        tgat(p, 0, sib, sib).wait_recv()
        for d in range(1, Z):
            other = lax.rem(zi + d, Z) * 2 + 1 - ci
            tgat(p, 0, other, sib).wait_recv()

        def text_take(i, carry):
            both = tg[p][:, :, i].astype(F32).reshape(S * G, 2 * TD, HD)
            for k in range(2):
                n.text[i, 2 * p + k] = (
                    both[:, k * TD : (k + 1) * TD].reshape(TEXT, HD).astype(BF16)
                )
            return carry

        lax.fori_loop(0, L, text_take, 0)

    lax.fori_loop(0, 1, video_pre, 0)
    send_slot(0)
    lax.fori_loop(1, 2, video_pre, 0)
    text_out(0)
    send_slot(1)
    lax.fori_loop(2, L, video_pre, 0)

    row = lax.broadcasted_iota(jnp.int32, (N, HD), 0)
    lane = lax.broadcasted_iota(jnp.int32, (N, HD), 1)
    tile_row = row // (N // 2)
    tile_col = lax.rem(row, GRID_W) // 8
    n.qaug[:, HD:] = jnp.where(lane == tile_row * 4 + tile_col, 1.0, 0.0).astype(BF16)

    def forward_halo(i):
        for d in range(1, G):
            inp_in(i, d).wait_recv()
        if i < 2:
            send_slot(2 * i + 2)
            send_slot(2 * i + 3)

        @pl.when(s < S - 1)
        def _():
            halo(i, True).start()

        @pl.when(s > 0)
        def _():
            halo(i, False).start()

    def key_rows(at, count, k_rows, v_rows, feature):
        n.kaug[at : at + count, :HD] = k_rows
        n.kaug[at : at + count, HD:] = feature
        n.vbuf[at : at + count, :] = v_rows

    def attend(i, chunks):
        reach_y = (n.table[x * L + i] >> 5) & 1
        reach_x = (n.table[x * L + i] >> 6) & 1
        fits = (jnp.abs(tile_row - lane // 4) <= reach_y) & (
            jnp.abs(tile_col - lax.rem(lane, 4)) <= reach_x
        )
        feature = jnp.where(fits, 0.0, NEGATIVE).astype(BF16)
        n.qaug[:, :HD] = n.recv[i, 0]
        key_rows(0, N, n.recv[i, 1], n.recv[i, 2], feature)
        key_rows(N, TEXT, n.text[i, 0], n.text[i, 1], n.tbias[...])
        if chunks > 3:
            for k, below in ((0, True), (1, False)):
                at = N + TEXT + k * N
                here = (s > 0) if below else (s < S - 1)

                @pl.when(here)
                def _():
                    halo_in(i, below).wait_recv()
                    key_rows(at, N, n.halo[i, k, 0], n.halo[i, k, 1], feature)

                @pl.when(jnp.logical_not(here))
                def _():
                    zero = jnp.zeros((N, HD), BF16)
                    key_rows(at, N, zero, zero, jnp.full((N, HD), NEGATIVE, BF16))

        for c in range(chunks):
            at = slice(c * 256, (c + 1) * 256)
            n.kT[:, at] = n.kaug[at, :HD].T
            n.vT[:, at] = n.vbuf[at, :].T

        def block(b, carry):
            at_q = pl.ds(pl.multiple_of(b * 256, 256), 256)
            qa = n.qaug[at_q, :]
            qn = n.qaug[at_q, :HD]
            gb = n.recv[i, 3, at_q, :]
            top = jnp.full((8, 256), NEGATIVE, F32)
            for c in range(chunks):
                at = slice(c * 256, (c + 1) * 256)
                sc = nt(n.kaug[at, :], qa)
                n.sbuf[at, :] = sc
                top = jnp.maximum(top, fold(sc, jnp.max))
            top = jnp.max(top, axis=0, keepdims=True) * SHARP
            total = jnp.zeros((8, 256), F32)
            acc = jnp.zeros((HD, 256), F32)
            for c in range(chunks):
                at = slice(c * 256, (c + 1) * 256)
                e = jnp.exp2(n.sbuf[at, :] * SHARP - top)
                n.sbuf[at, :] = e
                total = total + fold(e, jnp.sum)
                w = e.astype(BF16)
                acc = acc + nn(n.vT[:, at], w)
                dv = nn(w, gb)
                if c * 256 < N:
                    n.dvm[i, at, :] += dv
                elif c * 256 < N + TEXT:
                    n.dvt[i, :, :] += dv
                else:
                    n.dvh[c * 256 - N - TEXT : (c + 1) * 256 - N - TEXT, :] += dv
            inv = 1.0 / jnp.sum(total, axis=0, keepdims=True)
            out = (acc * inv).astype(BF16)
            gT = gb.astype(F32).T
            dot = jnp.sum(fold(gT * out.astype(F32), jnp.sum), axis=0, keepdims=True)
            dq = jnp.zeros((HD, 256), F32)
            for c in range(chunks):
                at = slice(c * 256, (c + 1) * 256)
                dp = nt(n.vbuf[at, :], gb)
                ds = ((n.sbuf[at, :] * inv) * (dp - dot)).astype(BF16)
                dq = dq + nn(n.kT[:, at], ds)
                dk = nn(ds, qn)
                if c * 256 < N:
                    n.dkm[i, at, :] += dk
                elif c * 256 < N + TEXT:
                    n.dkt[i, :, :] += dk
                else:
                    n.dkh[c * 256 - N - TEXT : (c + 1) * 256 - N - TEXT, :] += dk
            out = out.astype(F32).T.astype(BF16)
            dq = (dq * FACTOR).T.astype(BF16)
            for j in range(256 // R):
                n.osend[0, i, b * (256 // R) + j, 0] = out[j * R : (j + 1) * R]
                n.osend[0, i, b * (256 // R) + j, 1] = dq[j * R : (j + 1) * R]
            return carry

        n.dvm[i] = jnp.zeros((N, HD), F32)
        n.dkm[i] = jnp.zeros((N, HD), F32)
        n.dvt[i] = jnp.zeros((TEXT, HD), F32)
        n.dkt[i] = jnp.zeros((TEXT, HD), F32)
        if chunks > 3:
            n.dvh[...] = jnp.zeros((2 * N, HD), F32)
            n.dkh[...] = jnp.zeros((2 * N, HD), F32)
        lax.fori_loop(0, N // 256, block, 0)

        for d in range(1, G):
            outp(0, i, d).start()
        n.orecv[0][x * L + i] = n.osend[0, i, x]
        if chunks > 3:
            for k in range(2):
                n.hsend[i, k, 0] = (n.dkh[k * N : (k + 1) * N, :] * FACTOR).astype(BF16)
                n.hsend[i, k, 1] = n.dvh[k * N : (k + 1) * N, :].astype(BF16)

            @pl.when(s < S - 1)
            def _():
                hgrad(i, True).start()

            @pl.when(s > 0)
            def _():
                hgrad(i, False).start()

    share = pl.ds(pl.multiple_of(s * TS, TS), TS)
    share_bias = n.tbias[share, :].astype(F32)
    share_bias = jnp.concatenate([share_bias, share_bias], axis=1)

    def text_scores(i):
        sv = nt(n.recv[i, 1], n.text[i, 2])
        st = nt(n.text[i, 0, share, :], n.text[i, 2]) + share_bias
        pv = nt(n.recv[i, 2], n.text[i, 3])
        pt = nt(n.text[i, 1, share, :], n.text[i, 3])
        return sv, st, pv, pt

    def text_first(i, carry):
        sv, st, pv, pt = text_scores(i)
        top = jnp.maximum(fold(sv, jnp.max), fold(st, jnp.max))
        top = jnp.max(top, axis=0, keepdims=True)
        ev = jnp.exp2((sv - top) * SHARP)
        et = jnp.exp2((st - top) * SHARP)
        total = fold(ev, jnp.sum) + fold(et, jnp.sum)
        dot = fold(ev * pv, jnp.sum) + fold(et * pt, jnp.sum)
        n.stats[0, 0, pl.ds(i, 1), :] = top
        n.stats[0, 1, pl.ds(i, 1), :] = jnp.sum(total, axis=0, keepdims=True)
        n.stats[0, 2, pl.ds(i, 1), :] = jnp.sum(dot, axis=0, keepdims=True)
        return carry

    def text_second(i, carry):
        sv, st, pv, pt = text_scores(i)
        tops = [n.chips[k, 0, pl.ds(i, 1), :] for k in range(Z)]
        top = functools.reduce(jnp.maximum, tops)
        total = jnp.zeros((1, TEXT), F32)
        dot = jnp.zeros((1, TEXT), F32)
        for k in range(Z):
            scale = jnp.exp2((tops[k] - top) * SHARP)
            total = total + n.chips[k, 1, pl.ds(i, 1), :] * scale
            dot = dot + n.chips[k, 2, pl.ds(i, 1), :] * scale
        inv = 1.0 / total
        dot = dot * inv
        ev = jnp.exp2((sv - top) * SHARP)
        et = jnp.exp2((st - top) * SHARP)
        wv = ev.astype(BF16)
        wt = et.astype(BF16)
        dsv = (ev * inv * (pv - dot)).astype(BF16)
        dst = (et * inv * (pt - dot)).astype(BF16)
        qt_ = n.text[i, 2]
        gt_ = n.text[i, 3]
        n.dvm[i] += nn(wv, gt_)
        n.dkm[i] += nn(dsv, qt_)
        n.dvt[i, share, :] += nn(wt, gt_)
        n.dkt[i, share, :] += nn(dst, qt_)
        kt_ = n.recv[i, 1].T
        vt_ = n.recv[i, 2].T
        ktt = n.text[i, 0, share, :].astype(F32).T.astype(BF16)
        vtt = n.text[i, 1, share, :].astype(F32).T.astype(BF16)
        out = (nn(vt_, wv) + nn(vtt, wt)) * inv
        dq = (nn(kt_, dsv) + nn(ktt, dst)) * FACTOR
        n.tpart[:, 0, i] = out.T.astype(BF16).reshape(S, TS, HD)
        n.tpart[:, 1, i] = dq.T.astype(BF16).reshape(S, TS, HD)
        n.tpart[:, 2, i] = (n.dkt[i] * FACTOR).astype(BF16).reshape(S, TS, HD)
        n.tpart[:, 3, i] = n.dvt[i].astype(BF16).reshape(S, TS, HD)
        return carry

    def text_order(p, carry):
        h = order(p)
        n.rawp[0, p] = n.rawt[0, h]
        n.rawp[1, p] = n.rawt[1, h]
        return carry

    lax.fori_loop(0, HEADS, text_order, 0)
    forward_halo(0)
    text_relay(0)
    text_out(1)
    forward_halo(1)
    text_forward(0)
    text_in(0)

    def attend_pair(i, carry):
        attend(i, (3 * N + TEXT) // 256)

        @pl.when(i == 0)
        def _():
            forward_halo(2)
            text_relay(1)

        @pl.when(i == 1)
        def _():
            text_forward(1)

        for d in range(1, G):
            inp_in(LT + i, d).wait_recv()

        @pl.when(i == LT - 1)
        def _():
            text_in(1)
            n.stats[0] = jnp.zeros((3, 8, TEXT), F32)
            lax.fori_loop(0, L, text_first, 0)
            stat_pair().start()
            stat_pair().wait_recv()
            top = jnp.maximum(n.stats[0, 0], n.stats[1, 0])
            scales = [jnp.exp2((n.stats[k, 0] - top) * SHARP) for k in range(2)]
            n.chips[zi, 0] = top
            for a in (1, 2):
                n.chips[zi, a] = n.stats[0, a] * scales[0] + n.stats[1, a] * scales[1]
            for d in range(1, Z):
                stat(d).start()

        attend(LT + i, (N + TEXT) // 256)
        return carry

    lax.fori_loop(0, LT, attend_pair, 0)
    for d in range(1, Z):
        stat_in(d).wait_recv()

    def finish(i, wide):
        def pack(dk, dv):
            for j in range(G):
                n.osend[1, i, j, 0] = dk[j * R : (j + 1) * R].astype(BF16)
                n.osend[1, i, j, 1] = dv[j * R : (j + 1) * R].astype(BF16)

        if wide:
            for k, below in ((0, True), (1, False)):

                @pl.when((s > 0) if below else (s < S - 1))
                def _():
                    hgrad_in(i, below).wait_recv()
                    n.dkm[i] += n.hrecv[i, k, 0].astype(F32) * (1.0 / FACTOR)
                    n.dvm[i] += n.hrecv[i, k, 1].astype(F32)

        pack(n.dkm[i] * FACTOR, n.dvm[i])
        for d in range(1, G):
            outp(1, i, d).start()
        n.orecv[1][x * L + i] = n.osend[1, i, x]

    def finish_flat(i, carry):
        text_second(i, 0)
        finish(i, False)
        return carry

    def finish_wide(i, carry):
        finish(i, True)
        return carry

    def relay_sums():
        for k in range(2):
            to = lax.rem(zi + (1 if k == 0 else Z - 1), Z)
            rows = slice(2 * k, 2 * k + 2)
            zred(k).wait_recv()
            n.tz[to, rows] = (n.tz[to, rows].astype(F32) + n.tzh[k].astype(F32)).astype(BF16)
            zred(4 + k).start()

    lax.fori_loop(LT, L, finish_flat, 0)
    lax.fori_loop(0, LT, text_second, 0)
    for z in range(Z):
        pair(z).start()
    for z in range(Z):
        pair(z).wait_recv()
        n.tz[z] = (n.tpart[2 * z + ci].astype(F32) + n.tsib[z].astype(F32)).astype(BF16)
    for k in range(4):
        zred(k).start()
    lax.fori_loop(0, LT - 1, finish_wide, 0)
    relay_sums()
    lax.fori_loop(LT - 1, LT, finish_wide, 0)

    for i in range(L):
        for d in range(1, G):
            outp_in(0, i, d).wait_recv()

    def norm_back(u, dy, gain):
        f = u.astype(F32)
        r = inverse_rms(f)
        unit = f * r
        part = dy * unit
        return r * (dy * gain - unit * lane_mean(part * gain)), part

    cos_many = jnp.concatenate([n.cos[...]] * MANY, axis=0)
    sin_many = jnp.concatenate([n.sin[...]] * MANY, axis=0)

    def post(step, carry, received, back, plain, source, gain, out_plain, out_grad):
        heads = [MANY * step + k for k in range(MANY)]
        places = [place(h) for h in heads]
        for h, p in zip(heads, places):
            out_plain[:, lanes(h)] = received[p, plain]
        y = jnp.concatenate([received[p, back] for p in places], axis=0)
        u = jnp.concatenate([source[:, lanes(h)] for h in heads], axis=0)
        dy = y.astype(F32) * cos_many - nn(y, n.swap[...]) * sin_many
        grad, part = norm_back(u, dy, gain[...])
        for k, h in enumerate(heads):
            out_grad[:, lanes(h)] = grad[k * R : (k + 1) * R].astype(BF16)
        return carry + fold(part, jnp.sum)

    def post_q(step, carry):
        return post(step, carry, n.orecv[0], 1, 0, n.q, n.gqv, n.o_out, n.o_dq)

    def post_k(step, carry):
        return post(step, carry, n.orecv[1], 0, 1, n.k, n.gkv, n.o_dv, n.o_dk)

    zero = jnp.zeros((8, HD), F32)
    gain_qv = lax.fori_loop(0, HEADS // MANY, post_q, zero)

    for k in range(2, 6):
        zred(k).wait_recv()
    summed = n.tz[zi].astype(F32) + n.tzr[0].astype(F32) + n.tzr[1].astype(F32)
    for j in range(G):
        rows = slice(j * TD, (j + 1) * TD)
        for p in range(2):
            n.tfs[j, :, p] = jnp.concatenate(
                [summed[2 * p, :, rows], summed[2 * p + 1, :, rows]], axis=1
            ).astype(BF16)
    for d in range(1, G):
        tfin(d).start()
    n.tfr[pl.ds(x * L, L)] = n.tfs[x]

    for i in range(L):
        for d in range(1, G):
            outp_in(1, i, d).wait_recv()

    gain_kv = lax.fori_loop(0, HEADS // MANY, post_k, zero)

    for d in range(1, G):
        tfin_in(d).wait_recv()

    first = n.tfr[:, 0].astype(F32)
    second = n.tfr[:, 1].astype(F32)
    n.tres[0] = first[:, :TD]
    n.tres[3] = second[:, TD:]
    gain_t = []
    for k, dy, gain in ((0, first[:, TD:], n.gqt), (1, second[:, :TD], n.gkt)):
        u = n.rawp[k].reshape(HEADS * TD, HD)
        grad, part = norm_back(u, dy.reshape(HEADS * TD, HD), gain[...])
        n.tres[1 + k] = grad.reshape(HEADS, TD, HD)
        gain_t.append(fold(part, jnp.sum))

    def post_t(h, carry):
        p = place(h)
        n.o_outt[:, lanes(h)] = n.tres[0, p].astype(BF16)
        n.o_dqt[:, lanes(h)] = n.tres[1, p].astype(BF16)
        n.o_dkt[:, lanes(h)] = n.tres[2, p].astype(BF16)
        n.o_dvt[:, lanes(h)] = n.tres[3, p].astype(BF16)
        return carry

    parts = [
        jnp.sum(part, axis=0, keepdims=True) for part in (gain_qv, gain_kv, *gain_t)
    ]
    n.gx[0] = jnp.concatenate(parts + [jnp.zeros((4, HD), F32)], axis=0)
    for d in range(1, G):
        gainx(d).start()
    lax.fori_loop(0, HEADS, post_t, 0)
    for d in range(1, G):
        gainx(d).wait_recv()
    n.gs[0] = functools.reduce(lambda a, b: a + b, [n.gx[d] for d in range(G)])
    for d in range(1, S):
        gains(d).start()
    for d in range(1, S):
        gains(d).wait_recv()
    gain = functools.reduce(lambda a, b: a + b, [n.gs[d] for d in range(S)])
    n.o_gqv[...] = gain[0:1]
    n.o_gkv[...] = gain[1:2]
    n.o_gqt[...] = gain[2:3]
    n.o_gkt[...] = gain[3:4]

    for d in range(1, G):
        tx(0, d).wait_send()
        tx(1, d).wait_send()
        tfin(d).wait_send()
        gainx(d).wait_send()
        for i in range(L):
            inp(i, d).wait_send()
            outp(0, i, d).wait_send()
            outp(1, i, d).wait_send()
    for p in range(2):
        for sem in (0, 1, 2, 5, 6, 7):
            tgat(p, sem, s, sib).wait_send()
        for half in range(2):
            trelay(p, half, s, sib).wait_send()
    for k in range(6):
        zred(k).wait_send()
    for z in range(Z):
        pair(z).wait_send()
    stat_pair().wait_send()
    for d in range(1, Z):
        stat(d).wait_send()
    for d in range(1, S):
        gains(d).wait_send()
    for i in range(LT):
        for up in (True, False):

            @pl.when((s < S - 1) if up else (s > 0))
            def _():
                halo(i, up).wait_send()
                hgrad(i, up).wait_send()


def hand_on(count, *refs):
    held = refs[2 * count : 3 * count]
    sem = refs[-1]
    copies = [
        (
            pltpu.make_async_copy(refs[k], held[k], sem.at[0, k]),
            pltpu.make_async_copy(held[k], refs[count + k], sem.at[1, k]),
        )
        for k in range(count)
    ]
    for one, _ in copies:
        one.start()
    for one, two in copies:
        one.wait()
        two.start()
    for _, two in copies:
        two.wait()


def body(S, G, *args):
    (q, k, v, g, qt, kt, vt, gt, gqv, gkv, gqt, gkt, windows, text_mask) = args
    R = q.shape[0]
    TD = qt.shape[0]
    TS = TD * G
    N = R * G
    L = HEADS // G
    LT = L // 2
    Z = S // 2
    smem = pl.BlockSpec(memory_space=pltpu.SMEM)
    vmem = pl.BlockSpec(memory_space=pltpu.VMEM)
    operands = [
        ("table", head_order(windows, G), smem),
        ("tmask", text_mask.reshape(1, TEXT), vmem),
        ("gqv", gqv.reshape(1, HD), vmem),
        ("gkv", gkv.reshape(1, HD), vmem),
        ("gqt", gqt.reshape(1, HD), vmem),
        ("gkt", gkt.reshape(1, HD), vmem),
        ("q", q, vmem),
        ("k", k, vmem),
        ("v", v, vmem),
        ("g", g, vmem),
        ("qt", qt, vmem),
        ("kt", kt, vmem),
        ("vt", vt, vmem),
        ("gt", gt, vmem),
    ]
    rows = jax.ShapeDtypeStruct((R, D), BF16)
    trows = jax.ShapeDtypeStruct((TD, D), BF16)
    gain = jax.ShapeDtypeStruct((1, HD), F32)
    outs = [
        ("o_out", rows),
        ("o_outt", trows),
        ("o_dq", rows),
        ("o_dk", rows),
        ("o_dv", rows),
        ("o_dqt", trows),
        ("o_dkt", trows),
        ("o_dvt", trows),
        ("o_gqv", gain),
        ("o_gkv", gain),
        ("o_gqt", gain),
        ("o_gkt", gain),
    ]
    V = pltpu.VMEM
    dma = pltpu.SemaphoreType.DMA
    K = 3 * N + TEXT
    scratch = [
        ("raw", V((HEADS, 4, R, HD), BF16)),
        ("rawt", V((4, HEADS, TD, HD), F32)),
        ("normt", V((2, HEADS, TD, HD), F32)),
        ("rawp", V((2, HEADS, TD, HD), F32)),
        ("tres", V((4, HEADS, TD, HD), F32)),
        ("swap", V((HD, HD), BF16)),
        ("mean", V((2 * HD, HD), BF16)),
        ("cos", V((R, HD), F32)),
        ("sin", V((R, HD), F32)),
        ("gcos", V((2, R, HD), F32)),
        ("gsin", V((2, R, HD), F32)),
        ("tbias", V((TEXT, HD), BF16)),
        ("tsend", V((2, G, L, 2 * TD, HD), BF16)),
        ("tg0", V((S, G, L, 2 * TD, HD), BF16)),
        ("tg1", V((S, G, L, 2 * TD, HD), BF16)),
        ("text", V((L, 4, TEXT, HD), BF16)),
        ("send", V((L, G, 4, R, HD), BF16)),
        ("recv", V((L, 4, N, HD), BF16)),
        ("halo", V((LT, 2, 2, N, HD), BF16)),
        ("hsend", V((LT, 2, 2, N, HD), BF16)),
        ("hrecv", V((LT, 2, 2, N, HD), BF16)),
        ("osend", V((2, L, G, 2, R, HD), BF16)),
        ("orecv0", V((HEADS, 2, R, HD), BF16)),
        ("orecv1", V((HEADS, 2, R, HD), BF16)),
        ("stats", V((2, 3, 8, TEXT), F32)),
        ("chips", V((Z, 3, 8, TEXT), F32)),
        ("tpart", V((S, 4, L, TS, HD), BF16)),
        ("tsib", V((Z, 4, L, TS, HD), BF16)),
        ("tz", V((Z, 4, L, TS, HD), BF16)),
        ("tzr", V((2, 4, L, TS, HD), BF16)),
        ("tzh", V((2, 2, L, TS, HD), BF16)),
        ("tfs", V((G, L, 2, 2 * TD, HD), BF16)),
        ("tfr", V((HEADS, 2, 2 * TD, HD), BF16)),
        ("gx", V((G, 8, HD), F32)),
        ("gs", V((S, 8, HD), F32)),
        ("qaug", V((N, 2 * HD), BF16)),
        ("kaug", V((K, 2 * HD), BF16)),
        ("vbuf", V((K, HD), BF16)),
        ("kT", V((HD, K), BF16)),
        ("vT", V((HD, K), BF16)),
        ("sbuf", V((K, 256), F32)),
        ("dvm", V((L, N, HD), F32)),
        ("dkm", V((L, N, HD), F32)),
        ("dvt", V((L, TEXT, HD), F32)),
        ("dkt", V((L, TEXT, HD), F32)),
        ("dvh", V((2 * N, HD), F32)),
        ("dkh", V((2 * N, HD), F32)),
        ("tx_s", dma((2, G))),
        ("tx_r", dma((2, G))),
        ("tg_s", dma((2, 8))),
        ("tg_r", dma((2, S + 2))),
        ("in_s", dma((L, G))),
        ("in_r", dma((L, G))),
        ("ha_s", dma((LT, 2))),
        ("ha_r", dma((LT, 2))),
        ("hg_s", dma((LT, 2))),
        ("hg_r", dma((LT, 2))),
        ("o_s", dma((2, L, G))),
        ("o_r", dma((2, L, G))),
        ("st_s", dma((Z,))),
        ("st_r", dma((Z,))),
        ("p_s", dma((Z,))),
        ("p_r", dma((Z,))),
        ("z_s", dma((6,))),
        ("z_r", dma((6,))),
        ("tf_s", dma((G,))),
        ("tf_r", dma((G,))),
        ("gx_s", dma((G,))),
        ("gx_r", dma((G,))),
        ("gs_s", dma((S,))),
        ("gs_r", dma((S,))),
    ]
    names = [o[0] for o in operands] + [o[0] for o in outs] + [o[0] for o in scratch]
    result = pl.pallas_call(
        functools.partial(kernel, S, G, names),
        out_shape=[o[1] for o in outs],
        in_specs=[o[2] for o in operands],
        out_specs=[vmem] * len(outs),
        scratch_shapes=[o[1] for o in scratch],
        compiler_params=pltpu.CompilerParams(
            collective_id=0, has_side_effects=True, vmem_limit_bytes=50 << 20
        ),
        cost_estimate=pl.CostEstimate(
            flops=7 * 10**9, bytes_accessed=7 * 10**6, transcendentals=5 * 10**6
        ),
    )(*[o[1] for o in operands])
    here = pl.BlockSpec(memory_space=pl.ANY)
    result = pl.pallas_call(
        functools.partial(hand_on, len(outs)),
        out_shape=[o[1] for o in outs],
        in_specs=[here] * len(outs),
        out_specs=[here] * len(outs),
        scratch_shapes=[V(o[1].shape, o[1].dtype) for o in outs] + [dma((2, len(outs)))],
    )(*result)
    return tuple(result[:8]) + tuple(r.reshape(HD) for r in result[8:])


def solution(mesh):
    S = mesh.shape["slab"]
    G = mesh.shape["heads"]
    rows = P(("replica", "slab", "heads"), None)
    split = P("replica")
    return jax.shard_map(
        functools.partial(body, S, G),
        mesh=mesh,
        in_specs=(rows,) * 8 + (split,) * 4 + (P(), split),
        out_specs=(rows,) * 8 + (split,) * 4,
        check_vma=False,
    )
```
